32 devices in a mesh: tm: 8 (over z, y), space: 4 (over x, core).
Axes of the slice: x: 2, y: 2, z: 4, core: 2. Of those that a mesh axis runs over, the one named last changes fastest.
Arguments:
- start_states: float32 [8, 3, 16, 64, 256], P('tm', None, None, 'space'), may hold values from -6 to 6
- labels: int32 [16, 64, 256], P(None, 'space'), may hold values 0 or 1
Outputs:
- next_states: float32 [8, 3, 16, 64, 256], P('tm', None, None, 'space')
The draws below stay inside these ranges and needn't reach their ends.
All inputs are finite; a program needn't handle non-finite values. No bound on the sum of `labels` on one device may be relied on, other than what follows from the above.
Results may differ from the reference program's by a relative error of at most 0.0001.
Values sent between devices are 32-bit elements; how exact they have to be, the bound alone decides.
A program may use at most 128 MiB of HBM per device.

```python
import math
import jax
import jax.numpy as jnp
from jax import lax

NZ = 16
NY = 256
VCYCLES = 2
COARSE_SWEEPS = 4
NX = 64
N_TM = 8


def draw_start_states(key, part):
    keys = jax.random.split(jax.random.fold_in(key, 11), 3)
    columns = jnp.arange(NX, dtype=jnp.float32).reshape(1, 1, 1, NX, 1)
    phase = jax.random.uniform(keys[0], (N_TM, 3, 1, 1, 1), jnp.float32, 0.0, 2.0 * math.pi)
    sign = jnp.where(jax.random.bernoulli(keys[2], 0.5, (N_TM, 3, 1, 1, 1)), 1.0, -1.0).astype(jnp.float32)
    level = 1.5
    amplitude = 3.0
    coarse_noise = 0.7 * jnp.clip(jax.random.normal(keys[1], (N_TM, 3, NZ // 2, NX // 2, NY // 2), jnp.float32), -2.0, 2.0)
    noise = jnp.repeat(jnp.repeat(jnp.repeat(coarse_noise, 2, axis=2), 2, axis=3), 2, axis=4)
    wave = amplitude * jnp.sin(2.0 * math.pi * columns / 32.0 + phase)
    smooth = sign * level + wave
    return (jnp.broadcast_to(smooth, (N_TM, 3, NZ, NX, NY)) + noise).astype(jnp.float32)


def touch_ends(array, stream_key, smallest, top_value):
    dims = array.shape
    index_at = [jax.random.randint(jax.random.fold_in(stream_key, axis), (), 0, dims[axis]) for axis in range(len(dims))]
    array = array.at[tuple(index_at)].set(smallest)
    longest = dims.index(max(dims))
    index_at[longest] = (index_at[longest] + 1) % dims[longest]
    return array.at[tuple(index_at)].set(top_value)


def setup_inputs(seed: int = 0) -> dict:
    key_list = jax.random.split(jax.random.key(seed), 3)
    return {
        "start_states": draw_start_states(jax.random.fold_in(key_list[2], 71), 0),
        "labels": touch_ends((jax.random.randint(key_list[1], (NZ, NX, NY), 0, 20) < 1).astype(jnp.int32), jax.random.fold_in(key_list[1], 1), 0, 1),
    }


viscosity = 0.1
buoyancy = 0.2
relaxation = 0.8
coarse_rate = 0.15


def neighbour(values, direction, offset):
    position = values.ndim + direction
    padding = [(0, 0)] * values.ndim
    padding[position] = (1, 1)
    padded = jnp.pad(values, padding)
    length = values.shape[position]
    return lax.slice_in_dim(padded, 1 + offset, 1 + offset + length, axis=position)


def restrict(values):
    leading = values.shape[:-3]
    depth_cells, across_cells, height_cells = values.shape[-3:]
    shaped = values.reshape(leading + (depth_cells // 2, 2, across_cells // 2, 2, height_cells // 2, 2))
    return jnp.mean(shaped, axis=(-5, -3, -1))


def prolong(values):
    return jnp.repeat(jnp.repeat(jnp.repeat(values, 2, axis=-3), 2, axis=-2), 2, axis=-1)


def laplace_with(values, upper_across, lower_across):
    summed = neighbour(values, -3, 1) + neighbour(values, -3, -1) + upper_across + lower_across
    summed = summed + neighbour(values, -1, 1) + neighbour(values, -1, -1)
    return summed - 6.0 * values


def laplace(values):
    return laplace_with(values, neighbour(values, -2, 1), neighbour(values, -2, -1))


def face_weights(mobility, upper_across, lower_across):
    return ((0.5 * (mobility + neighbour(mobility, -3, 1)), 0.5 * (mobility + neighbour(mobility, -3, -1))),
            (0.5 * (mobility + upper_across), 0.5 * (mobility + lower_across)),
            (0.5 * (mobility + neighbour(mobility, -1, 1)), 0.5 * (mobility + neighbour(mobility, -1, -1))))


def scaled_weights(weights):
    return tuple((0.25 * upper_face, 0.25 * lower_face) for upper_face, lower_face in weights)


def weight_sum(weights):
    summed = weights[0][0] + weights[0][1]
    for upper_face, lower_face in weights[1:]:
        summed = summed + upper_face + lower_face
    return summed


def apply_weights(values, upper_across, lower_across, weights):
    depth_pair, across_pair, height_pair = weights
    summed = depth_pair[0] * (values - neighbour(values, -3, 1)) + depth_pair[1] * (values - neighbour(values, -3, -1))
    summed = summed + across_pair[0] * (values - upper_across) + across_pair[1] * (values - lower_across)
    return summed + height_pair[0] * (values - neighbour(values, -1, 1)) + height_pair[1] * (values - neighbour(values, -1, -1))


def operate(values, weights):
    return apply_weights(values, neighbour(values, -2, 1), neighbour(values, -2, -1), weights)


def vcycle(pressure, target, weights, diagonal, coarse_weights, coarse_diagonal):
    pressure = pressure + relaxation * (target - operate(pressure, weights)) / diagonal
    leftover = restrict(target - operate(pressure, weights))
    correction = relaxation * leftover / coarse_diagonal
    for sweep_number in range(COARSE_SWEEPS - 1):
        correction = correction + relaxation * (leftover - operate(correction, coarse_weights)) / coarse_diagonal
    pressure = pressure + prolong(correction)
    return pressure + relaxation * (target - operate(pressure, weights)) / diagonal


def fine_step(initial, mobility, weights, diagonal, coarse_weights, coarse_diagonal):
    zeros_field = jnp.zeros_like(mobility)
    predicted = initial + viscosity * laplace(initial) + jnp.stack([buoyancy * (2.0 * mobility - 1.0), zeros_field, zeros_field])
    spread = (neighbour(predicted[0], -3, 1) - neighbour(predicted[0], -3, -1)) + (neighbour(predicted[1], -2, 1) - neighbour(predicted[1], -2, -1))
    spread = spread + (neighbour(predicted[2], -1, 1) - neighbour(predicted[2], -1, -1))
    target = -0.5 * spread
    pressure = jnp.zeros_like(mobility)
    for cycle_number in range(VCYCLES):
        pressure = vcycle(pressure, target, weights, diagonal, coarse_weights, coarse_diagonal)
    gradient = jnp.stack([0.5 * (neighbour(pressure, -3, 1) - neighbour(pressure, -3, -1)),
                          0.5 * (neighbour(pressure, -2, 1) - neighbour(pressure, -2, -1)),
                          0.5 * (neighbour(pressure, -1, 1) - neighbour(pressure, -1, -1))])
    return predicted - mobility * gradient


def coarse_step(values, mobility_coarse):
    for substep in range(2):
        values = values + coarse_rate * mobility_coarse * laplace(values)
    return values


def reference(start_states, labels):
    mobility = 1.0 / (1.0 + 3.0 * labels.astype(jnp.float32))
    weights = face_weights(mobility, neighbour(mobility, -2, 1), neighbour(mobility, -2, -1))
    diagonal = weight_sum(weights)
    mobility_coarse = restrict(mobility)
    coarse_weights = scaled_weights(face_weights(mobility_coarse, neighbour(mobility_coarse, -2, 1), neighbour(mobility_coarse, -2, -1)))
    coarse_diagonal = weight_sum(coarse_weights)

    def slice_end(initial):
        return fine_step(initial, mobility, weights, diagonal, coarse_weights, coarse_diagonal)

    ends = lax.map(slice_end, start_states)

    def advance(carried, paired):
        initial, ending = paired
        coarse_end = restrict(ending)
        following = coarse_step(carried, mobility_coarse) + (coarse_end - coarse_step(restrict(initial), mobility_coarse))
        return following, ending + prolong(following - coarse_end)

    unused, next_states = lax.scan(advance, restrict(start_states[0]), (start_states, ends))
    return next_states
```

```python
import functools
import jax
import jax.numpy as jnp
from jax import lax
from jax.experimental import pallas as pl
from jax.experimental.pallas import tpu as pltpu
from jax.sharding import PartitionSpec as P

VISCOSITY = 0.1
BUOYANCY = 0.2
OMEGA = 0.8
RATE = 0.15
CYCLES = 2
SWEEPS = 4
H = 10
MESH = pl.DeviceIdType.MESH
f32 = jnp.float32


def split_dot(a, b):
    a1 = a.astype(jnp.bfloat16)
    rest = a - a1.astype(f32)
    a2 = rest.astype(jnp.bfloat16)
    a3 = (rest - a2.astype(f32)).astype(jnp.bfloat16)
    dot = functools.partial(jnp.dot, preferred_element_type=f32)
    return dot(a1, b) + (dot(a2, b) + dot(a3, b))


def shifts(v, zaxis, yaxis):
    nz, ny = v.shape[zaxis], v.shape[yaxis]
    return (
        pltpu.roll(v, nz - 1, zaxis),
        pltpu.roll(v, 1, zaxis),
        pltpu.roll(v, ny - 1, yaxis),
        pltpu.roll(v, 1, yaxis),
    )


def edge_masks(shape, zaxis, yaxis):
    z = lax.broadcasted_iota(jnp.int32, shape, zaxis)
    y = lax.broadcasted_iota(jnp.int32, shape, yaxis)
    return z < shape[zaxis] - 1, z > 0, y < shape[yaxis] - 1, y > 0


def masked_shifts(v, masks, zaxis, yaxis):
    return [jnp.where(m, s, 0.0) for m, s in zip(masks, shifts(v, zaxis, yaxis))]


def planes(lo, hi, fn, step=2):
    def some(k, carry):
        for j in range(step):
            fn(lo + k * step + j)
        return carry

    assert (hi - lo) % step == 0
    lax.fori_loop(0, (hi - lo) // step, some, 0)


def x_up(v):
    return jnp.concatenate([v[1:], jnp.zeros_like(v[:1])], axis=0)


def x_down(v):
    return jnp.concatenate([jnp.zeros_like(v[:1]), v[:-1]], axis=0)


def kernel(n, ntm, spans, u_in, m_in, out, u, m, pr, t, pa, pb, pc, rd, dg, wx, wzu, wzl, wyu, wyl,
           rs, rz, mc, cw, ce, mcw, csw, cew, gs, part, recv, wfin, down, dup,
           local_sem, us, ur, ms, mr, ts, tr, ps, pr_sem, mcs, mcr, css, csr, ces, cer, ss, sr, fs, fr):
    me, tm = lax.axis_index("space"), lax.axis_index("tm")
    X, Z, Y = u_in.shape[1:]
    Xc, Zc, Yc = X // 2, Z // 2, Y // 2
    HC = H // 2
    C = u_in.shape[0]
    has_left, has_right = me > 0, me < n - 1

    loads = [
        pltpu.make_async_copy(u_in, u.at[:, pl.ds(2, X)], local_sem.at[0]),
        pltpu.make_async_copy(m_in, m.at[pl.ds(H, X)], local_sem.at[1]),
    ]
    for c in loads:
        c.start()

    barrier = pltpu.get_barrier_semaphore()
    for k in range(1, n):
        pl.semaphore_signal(barrier, inc=1, device_id={"space": lax.rem(me + k, n)}, device_id_type=MESH)
    count = n - 1
    for s in spans:
        @pl.when(tm >= s)
        def _():
            pl.semaphore_signal(barrier, inc=1, device_id={"tm": tm - s}, device_id_type=MESH)

        @pl.when(tm + s < ntm)
        def _():
            pl.semaphore_signal(barrier, inc=1, device_id={"tm": tm + s}, device_id_type=MESH)

        count = count + jnp.where(tm >= s, 1, 0) + jnp.where(tm + s < ntm, 1, 0)

    @pl.when(jnp.logical_not(has_left))
    def _():
        u[:, 0:2] = jnp.zeros((C, 2, Z, Y), f32)
        for ref in (m, t, pb):
            ref[0:H] = jnp.zeros((H, Z, Y), f32)

    @pl.when(jnp.logical_not(has_right))
    def _():
        u[:, X + 2:X + 4] = jnp.zeros((C, 2, Z, Y), f32)
        for ref in (m, t, pb):
            ref[X + H:X + 2 * H] = jnp.zeros((H, Z, Y), f32)

    row = lax.broadcasted_iota(jnp.int32, (Y, Yc), 0)
    col = lax.broadcasted_iota(jnp.int32, (Y, Yc), 1)
    down[...] = jnp.where(lax.div(row, 2) == col, 0.125, 0.0).astype(jnp.bfloat16)
    row = lax.broadcasted_iota(jnp.int32, (Yc, Y), 0)
    col = lax.broadcasted_iota(jnp.int32, (Yc, Y), 1)
    dup[...] = jnp.where(row == lax.div(col, 2), 1.0, 0.0).astype(jnp.bfloat16)

    def restricted(count_c, plane_sum):
        def one(j, carry):
            rs[pl.ds(pl.multiple_of(j * Z, Z), Z), :] = plane_sum(j)
            return carry

        lax.fori_loop(0, count_c, one, 0)
        rows = count_c * Z
        rz[0:rows, :] = split_dot(rs[0:rows, :], down[...])
        half = rows // 2
        return (rz[pl.ds(0, half, stride=2), :] + rz[pl.ds(1, half, stride=2), :]).reshape(count_c, Zc, Yc)

    def prolonged(v):
        half = v.shape[0] * Zc
        flat = v.reshape(half, Yc)
        rz[pl.ds(0, half, stride=2), :] = flat
        rz[pl.ds(1, half, stride=2), :] = flat
        rs[0:2 * half, :] = split_dot(rz[0:2 * half, :], dup[...])

    def to_left(src, dst, ssem, rsem):
        return pltpu.make_async_remote_copy(src, dst, ssem, rsem, device_id={"space": me - 1}, device_id_type=MESH)

    def to_right(src, dst, ssem, rsem):
        return pltpu.make_async_remote_copy(src, dst, ssem, rsem, device_id={"space": me + 1}, device_id_type=MESH)

    class Exchange:
        def __init__(self, items, ssem, rsem):
            self.left, self.right = [], []
            for k, (at, first, width) in enumerate(items):
                self.left.append(to_left(at(first, width), at(first + X, width), ssem.at[0, k], rsem.at[0, k]))
                self.right.append(
                    to_right(at(first + X - width, width), at(first - width, width), ssem.at[1, k], rsem.at[1, k]))

        def start(self):
            @pl.when(has_left)
            def _():
                for c in self.left:
                    c.start()

            @pl.when(has_right)
            def _():
                for c in self.right:
                    c.start()

        def wait(self):
            @pl.when(has_left)
            def _():
                for c in self.left:
                    c.wait_send()
                for c in self.right:
                    c.wait_recv()

            @pl.when(has_right)
            def _():
                for c in self.right:
                    c.wait_send()
                for c in self.left:
                    c.wait_recv()

    def plane_view(ref):
        return lambda first, width: ref.at[pl.ds(first, width)]

    for c in loads:
        c.wait()
    pl.semaphore_wait(barrier, count)

    u_x = Exchange([(lambda f, w, d=d: u.at[d, pl.ds(f, w)], 2, 2 if d == 1 else 1) for d in range(C)], us, ur)
    m_x = Exchange([(plane_view(m), H, H)], ms, mr)
    t_x = Exchange([(plane_view(t), H, H - 1)], ts, tr)
    p_x = Exchange([(plane_view(pb), H, H)], ps, pr_sem)
    u_x.start()
    m_x.start()

    def own_rows(ref):
        return ref.at[pl.ds(me * Xc, Xc)]

    mine = restricted(Xc, lambda j: m[H + 2 * j] + m[H + 2 * j + 1])
    mc[HC:HC + Xc] = mine
    mcw[pl.ds(me * Xc, Xc)] = mine
    for d in range(C):
        gs[d] = restricted(Xc, lambda j: u[d, 2 + 2 * j] + u[d, 3 + 2 * j])

    def mc_copy(k, src):
        peer = lax.rem(me + k, n)
        at = mc.at[pl.ds(HC, Xc)]
        return pltpu.make_async_remote_copy(
            at, mcw.at[pl.ds(src * Xc, Xc)], mcs.at[k], mcr.at[k], device_id={"space": peer}, device_id_type=MESH)

    for k in range(1, n):
        mc_copy(k, me).start()

    def gather_copy(src, dst, d, ssem, rsem, sender):
        return pltpu.make_async_remote_copy(
            src.at[d], dst.at[pl.ds(sender * Xc, Xc)], ssem.at[d], rsem.at[sender],
            device_id={"space": d}, device_id_type=MESH)

    def gather_start(src, dst, ssem, rsem):
        for d in range(C):
            @pl.when(me == d)
            def _():
                dst[pl.ds(d * Xc, Xc)] = src[d]

            @pl.when(me != d)
            def _():
                gather_copy(src, dst, d, ssem, rsem, me).start()

    def gather_wait_recv(src, dst, ssem, rsem):
        for sender in range(n):
            @pl.when(me != sender)
            def _():
                gather_copy(src, dst, 0, ssem, rsem, sender).wait_recv()

    def gather_wait_send(src, dst, ssem, rsem):
        for d in range(C):
            @pl.when(me != d)
            def _():
                gather_copy(src, dst, d, ssem, rsem, me).wait_send()

    gather_start(gs, csw, css, csr)

    fine_masks = edge_masks((Z, Y), 0, 1)

    def lap(d, i):
        v = u[d, i]
        summed = u[d, i - 1] + u[d, i + 1]
        zu, zl, yu, yl = masked_shifts(v, fine_masks, 0, 1)
        summed = summed + (zu + zl) + (yu + yl)
        return v + VISCOSITY * (summed - 6.0 * v)

    u_x.wait()

    def predict(i):
        pr[0, i] = lap(0, i + 1) + BUOYANCY * (2.0 * m[i - 1 + H] - 1.0)
        pr[1, i] = lap(1, i + 1)
        pr[2, i] = lap(2, i + 1)

    planes(1, X + 1, predict)
    pr[1, 0] = jnp.where(has_left, lap(1, 1), 0.0)
    pr[1, X + 1] = jnp.where(has_right, lap(1, X + 2), 0.0)

    def aim(i):
        zu, zl, _, _ = masked_shifts(pr[0, i], fine_masks, 0, 1)
        _, _, yu, yl = masked_shifts(pr[2, i], fine_masks, 0, 1)
        t[i - 1 + H] = -0.5 * ((zu - zl) + (pr[1, i + 1] - pr[1, i - 1]) + (yu - yl))

    planes(1, X + 1, aim)
    t_x.start()

    m_x.wait()

    def weigh(i):
        v = m[i]
        up, low = 0.5 * (v + m[i + 1]), 0.5 * (v + m[i - 1])
        wx[i] = up
        total = up + low
        for ref, mask, s in zip((wzu, wzl, wyu, wyl), fine_masks, shifts(v, 0, 1)):
            total = total + 0.5 * (v + jnp.where(mask, s, 0.0))
            ref[i] = jnp.where(mask, 0.5 * (v + s), 0.0)
        dg[i] = total
        rd[i] = jnp.where(v > 0.0, OMEGA / jnp.where(v > 0.0, total, 1.0), 0.0)

    wx[0] = 0.5 * (m[0] + m[1])
    planes(1, X + 2 * H - 1, weigh)

    mc[0:HC] = restricted(HC, lambda j: m[2 * j] + m[2 * j + 1])
    mc[HC + Xc:] = restricted(HC, lambda j: m[H + X + 2 * j] + m[H + X + 2 * j + 1])
    W = Xc + 2 * HC - 2
    mid = mc[1:1 + W]
    coarse_masks = edge_masks((W, Zc, Yc), 1, 2)
    cw[0] = 0.125 * (mid + mc[2:2 + W])
    cw[1] = 0.125 * (mid + mc[0:W])
    total = cw[0] + cw[1]
    for k, (mask, s) in enumerate(zip(coarse_masks, shifts(mid, 1, 2))):
        total = total + 0.125 * (mid + jnp.where(mask, s, 0.0))
        cw[2 + k] = jnp.where(mask, 0.125 * (mid + s), 0.0)
    cw[6] = jnp.where(mid > 0.0, OMEGA / jnp.where(mid > 0.0, total, 1.0), 0.0)

    def flux(p, i):
        v = p[i]
        zu, zl, yu, yl = shifts(v, 0, 1)
        s = wx[i] * p[i + 1] + wx[i - 1] * p[i - 1]
        s = s + (wzu[i] * zu + wzl[i] * zl)
        return v, s + (wyu[i] * yu + wyl[i] * yl)

    def smooth(src, dst, width):
        def one(i):
            v, s = flux(src, i)
            dst[i] = (1.0 - OMEGA) * v + rd[i] * (t[i] + s)

        planes(H - width, H + X + width, one)

    def residual(p, i):
        v, s = flux(p, i)
        return t[i] - dg[i] * v + s

    def coarse_correct(p, extra):
        first = H - 2 * (HC - 1)
        left = restricted(W, lambda j: residual(p, first + 2 * j) + residual(p, first + 2 * j + 1))
        v = cw[6] * left
        for _ in range(SWEEPS - 1):
            zu, zl, yu, yl = shifts(v, 1, 2)
            s = cw[0] * x_up(v) + cw[1] * x_down(v) + (cw[2] * zu + cw[3] * zl) + (cw[4] * yu + cw[5] * yl)
            v = (1.0 - OMEGA) * v + cw[6] * (left + s)
        prolonged(v[HC - 2:W - (HC - 2)])

        def add(j, carry):
            c = rs[pl.ds(pl.multiple_of(j * Z, Z), Z), :]
            for h in range(2):
                p[H - 2 + 2 * j + h] = p[H - 2 + 2 * j + h] + c
            return carry

        lax.fori_loop(0, Xc + 2, add, 0)

    t_x.wait()

    def first_guess(i):
        pa[i] = rd[i] * t[i]

    planes(1, X + 2 * H - 1, first_guess)
    coarse_correct(pa, 0)
    smooth(pa, pb, 0)
    p_x.start()

    grid_masks = edge_masks((n * Xc, Zc, Yc), 1, 2)

    def substep(v):
        a = mcw[...] * RATE
        zu, zl, yu, yl = masked_shifts(v, grid_masks, 1, 2)
        s = x_up(v) + x_down(v) + (zu + zl) + (yu + yl)
        return v + a * (s - 6.0 * v)

    def steps(ref, times):
        def one(k, carry):
            ref[...] = substep(ref[...])
            return carry

        lax.fori_loop(0, 2 * times, one, 0)

    for k in range(1, n):
        mc_copy(k, lax.rem(me + n - k, n)).wait_recv()

    @pl.when(me < C)
    def _():
        gather_wait_recv(gs, csw, css, csr)
        steps(csw, 1)

    p_x.wait()
    smooth(pb, pa, H - 1)
    coarse_correct(pa, 1)
    smooth(pa, pc, 1)

    def finish(i):
        v = pc[i]
        zu, zl, yu, yl = masked_shifts(v, fine_masks, 0, 1)
        k = i - H + 1
        half = 0.5 * m[i]
        out[0, i - H] = pr[0, k] - half * (zu - zl)
        out[1, i - H] = pr[1, k] - half * (pc[i + 1] - pc[i - 1])
        out[2, i - H] = pr[2, k] - half * (yu - yl)

    planes(H, H + X, finish)
    for d in range(C):
        ce[d] = restricted(Xc, lambda j: out[d, 2 * j] + out[d, 2 * j + 1])
    gather_start(ce, cew, ces, cer)

    def final_copy(d, peer):
        return pltpu.make_async_remote_copy(
            part.at[len(spans), pl.ds(peer * Xc, Xc)], wfin.at[d], fs.at[peer], fr.at[d],
            device_id={"space": peer}, device_id_type=MESH)

    @pl.when(me < C)
    def _():
        gather_wait_recv(ce, cew, ces, cer)
        part[0] = jnp.where(tm == 0, cew[...], cew[...] - csw[...])
        for r, s in enumerate(spans):
            def hop(target):
                return pltpu.make_async_remote_copy(
                    part.at[r], recv.at[r], ss.at[r], sr.at[r], device_id={"tm": target}, device_id_type=MESH)

            @pl.when(tm + s < ntm)
            def _():
                hop(tm + s).start()

            @pl.when(tm >= s)
            def _():
                hop(tm).wait_recv()
                steps(recv.at[r], s)
                part[r + 1] = part[r] + recv[r]

            @pl.when(tm < s)
            def _():
                part[r + 1] = part[r]

        for peer in range(n):
            @pl.when(me != peer)
            def _():
                final_copy(me, peer).start()

            @pl.when(me == peer)
            def _():
                wfin[peer if peer < C else 0] = part[len(spans), pl.ds(peer * Xc, Xc)]

    for d in range(C):
        @pl.when(me != d)
        def _():
            final_copy(d, d).wait_recv()

        prolonged(wfin[d] - ce[d])

        def add(j, carry):
            c = rs[pl.ds(pl.multiple_of(j * Z, Z), Z), :]
            for h in range(2):
                out[d, 2 * j + h] = out[d, 2 * j + h] + c
            return carry

        lax.fori_loop(0, Xc, add, 0)

    for k in range(1, n):
        mc_copy(k, me).wait_send()
    gather_wait_send(gs, csw, css, csr)
    gather_wait_send(ce, cew, ces, cer)

    @pl.when(me < C)
    def _():
        for r, s in enumerate(spans):
            @pl.when(tm + s < ntm)
            def _():
                pltpu.make_async_remote_copy(
                    part.at[r], recv.at[r], ss.at[r], sr.at[r],
                    device_id={"tm": tm + s}, device_id_type=MESH).wait_send()
        for peer in range(n):
            @pl.when(me != peer)
            def _():
                final_copy(me, peer).wait_send()


def body(n, ntm, start_states, labels):
    C, Z, X, Y = start_states.shape[1:]
    Xc, Zc, Yc = X // 2, Z // 2, Y // 2
    HC = H // 2
    spans = []
    while (1 << len(spans)) < ntm:
        spans.append(1 << len(spans))
    mobility = 1.0 / (1.0 + 3.0 * labels.astype(f32))
    u_in = jnp.swapaxes(start_states[0], 1, 2)
    m_in = jnp.swapaxes(mobility, 0, 1)
    wide = pltpu.VMEM((X + 2 * H, Z, Y), f32)
    W = Xc + 2 * HC - 2
    grid = pltpu.VMEM((n * Xc, Zc, Yc), f32)
    rows = max(W, Xc + 2) * Z
    R = len(spans)
    dma = pltpu.SemaphoreType.DMA
    scratch = [
        pltpu.VMEM((C, X + 4, Z, Y), f32), wide, pltpu.VMEM((C, X + 2, Z, Y), f32),
        wide, wide, wide, wide, wide, wide, wide, wide, wide, wide, wide,
        pltpu.VMEM((rows, Y), f32), pltpu.VMEM((rows, Yc), f32),
        pltpu.VMEM((Xc + 2 * HC, Zc, Yc), f32), pltpu.VMEM((7, W, Zc, Yc), f32),
        pltpu.VMEM((C, Xc, Zc, Yc), f32), grid, grid, grid, pltpu.VMEM((C, Xc, Zc, Yc), f32),
        pltpu.VMEM((R + 1, n * Xc, Zc, Yc), f32), pltpu.VMEM((max(R, 1), n * Xc, Zc, Yc), f32),
        pltpu.VMEM((C, Xc, Zc, Yc), f32),
        pltpu.VMEM((Y, Yc), jnp.bfloat16), pltpu.VMEM((Yc, Y), jnp.bfloat16),
        dma((2,)), dma((2, C)), dma((2, C)), dma((2, 1)), dma((2, 1)), dma((2, 1)), dma((2, 1)),
        dma((2, 1)), dma((2, 1)), dma((n,)), dma((n,)), dma((C,)), dma((n,)), dma((C,)), dma((n,)),
        dma((max(R, 1),)), dma((max(R, 1),)), dma((n,)), dma((C,)),
    ]
    result = pl.pallas_call(
        functools.partial(kernel, n, ntm, spans),
        out_shape=jax.ShapeDtypeStruct((C, X, Z, Y), f32),
        in_specs=[pl.BlockSpec(memory_space=pl.ANY)] * 2,
        out_specs=pl.BlockSpec(memory_space=pltpu.VMEM),
        scratch_shapes=scratch,
        compiler_params=pltpu.CompilerParams(
            collective_id=0, has_side_effects=True, vmem_limit_bytes=40 * 1024 * 1024),
    )(u_in, m_in)
    return jnp.swapaxes(result, 1, 2)[None]


def solution(mesh):
    in_specs = (P("tm", None, None, "space", None), P(None, "space", None))
    out_specs = P("tm", None, None, "space", None)
    fn = functools.partial(body, mesh.shape["space"], mesh.shape["tm"])
    return jax.shard_map(fn, mesh=mesh, in_specs=in_specs, out_specs=out_specs, check_vma=False)
```

```python
import functools
import jax
import jax.numpy as jnp
from jax import lax
from jax.experimental import pallas as pl
from jax.experimental.pallas import tpu as pltpu
from jax.sharding import PartitionSpec as P

VISCOSITY = 0.1
BUOYANCY = 0.2
OMEGA = 0.8
RATE = 0.15
CYCLES = 2
SWEEPS = 4
H = 10
MESH = pl.DeviceIdType.MESH
f32 = jnp.float32


def split_dot(a, b):
    a1 = a.astype(jnp.bfloat16)
    rest = a - a1.astype(f32)
    a2 = rest.astype(jnp.bfloat16)
    a3 = (rest - a2.astype(f32)).astype(jnp.bfloat16)
    dot = functools.partial(jnp.dot, preferred_element_type=f32)
    return dot(a1, b) + (dot(a2, b) + dot(a3, b))


def shifts(v, zaxis, yaxis):
    nz, ny = v.shape[zaxis], v.shape[yaxis]
    return (
        pltpu.roll(v, nz - 1, zaxis),
        pltpu.roll(v, 1, zaxis),
        pltpu.roll(v, ny - 1, yaxis),
        pltpu.roll(v, 1, yaxis),
    )


def edge_masks(shape, zaxis, yaxis):
    z = lax.broadcasted_iota(jnp.int32, shape, zaxis)
    y = lax.broadcasted_iota(jnp.int32, shape, yaxis)
    return z < shape[zaxis] - 1, z > 0, y < shape[yaxis] - 1, y > 0


def masked_shifts(v, masks, zaxis, yaxis):
    return [jnp.where(m, s, 0.0) for m, s in zip(masks, shifts(v, zaxis, yaxis))]


def planes(lo, hi, fn, step=8):
    def some(k, carry):
        for j in range(step):
            fn(lo + k * step + j)
        return carry

    turns = (hi - lo) // step
    if turns > 1:
        lax.fori_loop(0, turns, some, 0)
        lo = lo + turns * step
    for i in range(lo, hi):
        fn(i)


def rows_at(j, size):
    return pl.ds(j * size if isinstance(j, int) else pl.multiple_of(j * size, size), size)


def x_up(v):
    return jnp.concatenate([v[1:], jnp.zeros_like(v[:1])], axis=0)


def x_down(v):
    return jnp.concatenate([jnp.zeros_like(v[:1]), v[:-1]], axis=0)


def kernel(n, ntm, spans, u_in, l_in, out, u_raw, l_raw, u, m, pr, t, pa, pb, pc, rd, dg, wx, wzu, wzl, wyu, wyl,
           rs, rz, mc, cw, ce, mcw, csw, cew, gs, part, recv, wfin, down, dup,
           local_sem, us, ur, ms, mr, ts, tr, ps, pr_sem, mcs, mcr, css, csr, ces, cer, ss, sr, fs, fr):
    me, tm = lax.axis_index("space"), lax.axis_index("tm")
    Z, X, Y = u_in.shape[1:]
    Xc, Zc, Yc = X // 2, Z // 2, Y // 2
    HC = H // 2
    C = u_in.shape[0]
    has_left, has_right = me > 0, me < n - 1

    loads = [
        pltpu.make_async_copy(u_in, u_raw, local_sem.at[0]),
        pltpu.make_async_copy(l_in, l_raw, local_sem.at[1]),
    ]
    for c in loads:
        c.start()

    barrier = pltpu.get_barrier_semaphore()
    for k in range(1, n):
        pl.semaphore_signal(barrier, inc=1, device_id={"space": lax.rem(me + k, n)}, device_id_type=MESH)
    count = n - 1
    for s in spans:
        @pl.when(tm >= s)
        def _():
            pl.semaphore_signal(barrier, inc=1, device_id={"tm": tm - s}, device_id_type=MESH)

        @pl.when(tm + s < ntm)
        def _():
            pl.semaphore_signal(barrier, inc=1, device_id={"tm": tm + s}, device_id_type=MESH)

        count = count + jnp.where(tm >= s, 1, 0) + jnp.where(tm + s < ntm, 1, 0)

    @pl.when(jnp.logical_not(has_left))
    def _():
        u[:, 0:2] = jnp.zeros((C, 2, Z, Y), f32)
        for ref in (m, t, pb):
            ref[0:H] = jnp.zeros((H, Z, Y), f32)

    @pl.when(jnp.logical_not(has_right))
    def _():
        u[:, X + 2:X + 4] = jnp.zeros((C, 2, Z, Y), f32)
        for ref in (m, t, pb):
            ref[X + H:X + 2 * H] = jnp.zeros((H, Z, Y), f32)

    row = lax.broadcasted_iota(jnp.int32, (Y, Yc), 0)
    col = lax.broadcasted_iota(jnp.int32, (Y, Yc), 1)
    down[...] = jnp.where(lax.div(row, 2) == col, 0.125, 0.0).astype(jnp.bfloat16)
    row = lax.broadcasted_iota(jnp.int32, (Yc, Y), 0)
    col = lax.broadcasted_iota(jnp.int32, (Yc, Y), 1)
    dup[...] = jnp.where(row == lax.div(col, 2), 1.0, 0.0).astype(jnp.bfloat16)

    def fill(lo, hi, plane_sum, base=0):
        def one(j):
            rs[rows_at(base + j, Z), :] = plane_sum(j)

        planes(lo, hi, one, 4)

    def restricted(count_c, plane_sum):
        fill(0, count_c, plane_sum)
        return averaged(count_c)

    def averaged(count_c):
        rows = count_c * Z
        rz[0:rows, :] = split_dot(rs[0:rows, :], down[...])
        half = rows // 2
        return (rz[pl.ds(0, half, stride=2), :] + rz[pl.ds(1, half, stride=2), :]).reshape(count_c, Zc, Yc)

    def prolonged(v):
        half = v.shape[0] * Zc
        flat = v.reshape(half, Yc)
        rz[pl.ds(0, half, stride=2), :] = flat
        rz[pl.ds(1, half, stride=2), :] = flat
        rs[0:2 * half, :] = split_dot(rz[0:2 * half, :], dup[...])

    def to_left(src, dst, ssem, rsem):
        return pltpu.make_async_remote_copy(src, dst, ssem, rsem, device_id={"space": me - 1}, device_id_type=MESH)

    def to_right(src, dst, ssem, rsem):
        return pltpu.make_async_remote_copy(src, dst, ssem, rsem, device_id={"space": me + 1}, device_id_type=MESH)

    class Exchange:
        def __init__(self, items, ssem, rsem):
            self.left, self.right = [], []
            for k, (at, first, width) in enumerate(items):
                self.left.append(to_left(at(first, width), at(first + X, width), ssem.at[0, k], rsem.at[0, k]))
                self.right.append(
                    to_right(at(first + X - width, width), at(first - width, width), ssem.at[1, k], rsem.at[1, k]))

        def start(self):
            @pl.when(has_left)
            def _():
                for c in self.left:
                    c.start()

            @pl.when(has_right)
            def _():
                for c in self.right:
                    c.start()

        def wait(self):
            @pl.when(has_left)
            def _():
                for c in self.left:
                    c.wait_send()
                for c in self.right:
                    c.wait_recv()

            @pl.when(has_right)
            def _():
                for c in self.right:
                    c.wait_send()
                for c in self.left:
                    c.wait_recv()

    def plane_view(ref):
        return lambda first, width: ref.at[pl.ds(first, width)]

    loads[0].wait()
    for d in range(C):
        u[d, 2:2 + X] = jnp.swapaxes(u_raw[d], 0, 1)
    loads[1].wait()
    m[H:H + X] = jnp.swapaxes(1.0 - 0.75 * l_raw[...].astype(f32), 0, 1)
    pl.semaphore_wait(barrier, count)

    u_x = Exchange([(lambda f, w, d=d: u.at[d, pl.ds(f, w)], 2, 2 if d == 1 else 1) for d in range(C)], us, ur)
    m_x = Exchange([(plane_view(m), H, H)], ms, mr)
    t_x = Exchange([(plane_view(t), H, H - 1)], ts, tr)
    p_x = Exchange([(plane_view(pb), H, H)], ps, pr_sem)
    u_x.start()
    m_x.start()

    def own_rows(ref):
        return ref.at[pl.ds(me * Xc, Xc)]

    mine = restricted(Xc, lambda j: m[H + 2 * j] + m[H + 2 * j + 1])
    mc[HC:HC + Xc] = mine
    mcw[pl.ds(me * Xc, Xc)] = mine
    for d in range(C):
        fill(0, Xc, lambda j: u[d, 2 + 2 * j] + u[d, 3 + 2 * j], d * Xc)
    gs[...] = averaged(C * Xc).reshape(C, Xc, Zc, Yc)

    def mc_copy(k, src):
        peer = lax.rem(me + k, n)
        at = mc.at[pl.ds(HC, Xc)]
        return pltpu.make_async_remote_copy(
            at, mcw.at[pl.ds(src * Xc, Xc)], mcs.at[k], mcr.at[k], device_id={"space": peer}, device_id_type=MESH)

    def gather_copy(src, dst, d, ssem, rsem, sender):
        return pltpu.make_async_remote_copy(
            src.at[d], dst.at[pl.ds(sender * Xc, Xc)], ssem.at[d], rsem.at[sender],
            device_id={"space": d}, device_id_type=MESH)

    def gather_start(src, dst, ssem, rsem):
        for d in range(C):
            @pl.when(me == d)
            def _():
                dst[pl.ds(d * Xc, Xc)] = src[d]

            @pl.when(me != d)
            def _():
                gather_copy(src, dst, d, ssem, rsem, me).start()

    def gather_wait_recv(src, dst, ssem, rsem):
        for sender in range(n):
            @pl.when(me != sender)
            def _():
                gather_copy(src, dst, 0, ssem, rsem, sender).wait_recv()

    def gather_wait_send(src, dst, ssem, rsem):
        for d in range(C):
            @pl.when(me != d)
            def _():
                gather_copy(src, dst, d, ssem, rsem, me).wait_send()

    fine_masks = edge_masks((Z, Y), 0, 1)

    def lap(d, i):
        v = u[d, i]
        summed = u[d, i - 1] + u[d, i + 1]
        zu, zl, yu, yl = masked_shifts(v, fine_masks, 0, 1)
        summed = summed + (zu + zl) + (yu + yl)
        return v + VISCOSITY * (summed - 6.0 * v)

    u_x.wait()

    def predict(i):
        pr[0, i] = lap(0, i + 1) + BUOYANCY * (2.0 * m[i - 1 + H] - 1.0)
        pr[1, i] = lap(1, i + 1)
        pr[2, i] = lap(2, i + 1)

    planes(1, X + 1, predict)
    pr[1, 0] = jnp.where(has_left, lap(1, 1), 0.0)
    pr[1, X + 1] = jnp.where(has_right, lap(1, X + 2), 0.0)

    def aim(i):
        zu, zl, _, _ = masked_shifts(pr[0, i], fine_masks, 0, 1)
        _, _, yu, yl = masked_shifts(pr[2, i], fine_masks, 0, 1)
        t[i - 1 + H] = -0.5 * ((zu - zl) + (pr[1, i + 1] - pr[1, i - 1]) + (yu - yl))

    planes(1, X + 1, aim)
    t_x.start()

    m_x.wait()

    def weigh(i):
        v = m[i]
        up, low = 0.5 * (v + m[i + 1]), 0.5 * (v + m[i - 1])
        wx[i] = up
        total = up + low
        for ref, mask, s in zip((wzu, wzl, wyu, wyl), fine_masks, shifts(v, 0, 1)):
            total = total + 0.5 * (v + jnp.where(mask, s, 0.0))
            ref[i] = jnp.where(mask, 0.5 * (v + s), 0.0)
        dg[i] = total
        rd[i] = jnp.where(v > 0.0, OMEGA / jnp.where(v > 0.0, total, 1.0), 0.0)

    wx[0] = 0.5 * (m[0] + m[1])
    planes(1, X + 2 * H - 1, weigh)

    mc[0:HC] = restricted(HC, lambda j: m[2 * j] + m[2 * j + 1])
    mc[HC + Xc:] = restricted(HC, lambda j: m[H + X + 2 * j] + m[H + X + 2 * j + 1])
    W = Xc + 2 * HC - 2
    mid = mc[1:1 + W]
    coarse_masks = edge_masks((W, Zc, Yc), 1, 2)
    cw[0] = 0.125 * (mid + mc[2:2 + W])
    cw[1] = 0.125 * (mid + mc[0:W])
    total = cw[0] + cw[1]
    for k, (mask, s) in enumerate(zip(coarse_masks, shifts(mid, 1, 2))):
        total = total + 0.125 * (mid + jnp.where(mask, s, 0.0))
        cw[2 + k] = jnp.where(mask, 0.125 * (mid + s), 0.0)
    cw[6] = jnp.where(mid > 0.0, OMEGA / jnp.where(mid > 0.0, total, 1.0), 0.0)

    def flux(p, i):
        v = p[i]
        zu, zl, yu, yl = shifts(v, 0, 1)
        s = wx[i] * p[i + 1] + wx[i - 1] * p[i - 1]
        s = s + (wzu[i] * zu + wzl[i] * zl)
        return v, s + (wyu[i] * yu + wyl[i] * yl)

    def smooth(src, dst, lo, hi):
        def one(i):
            v, s = flux(src, i)
            dst[i] = (1.0 - OMEGA) * v + rd[i] * (t[i] + s)

        planes(lo, hi, one)

    def residual(p, i):
        v, s = flux(p, i)
        return t[i] - dg[i] * v + s

    first = H - 2 * (HC - 1)

    def leftover(p, lo, hi):
        fill(lo, hi, lambda j: residual(p, first + 2 * j) + residual(p, first + 2 * j + 1))

    def coarse_correct(p):
        left = averaged(W)
        v = cw[6] * left
        for _ in range(SWEEPS - 1):
            zu, zl, yu, yl = shifts(v, 1, 2)
            s = cw[0] * x_up(v) + cw[1] * x_down(v) + (cw[2] * zu + cw[3] * zl) + (cw[4] * yu + cw[5] * yl)
            v = (1.0 - OMEGA) * v + cw[6] * (left + s)
        prolonged(v[HC - 2:W - (HC - 2)])

        def add(j):
            c = rs[rows_at(j, Z), :]
            for h in range(2):
                p[H - 2 + 2 * j + h] = p[H - 2 + 2 * j + h] + c

        planes(0, Xc + 2, add, 5)

    t_x.wait()
    for k in range(1, n):
        mc_copy(k, me).start()
    gather_start(gs, csw, css, csr)

    def first_guess(i):
        pa[i] = rd[i] * t[i]

    planes(1, X + 2 * H - 1, first_guess)
    leftover(pa, 0, W)
    coarse_correct(pa)
    smooth(pa, pb, H, H + X)
    p_x.start()

    smooth(pb, pa, H + 1, H + X - 1)
    leftover(pa, HC, HC + Xc - 2)
    grid_masks = edge_masks((n * Xc, Zc, Yc), 1, 2)

    def substep(v):
        a = mcw[...] * RATE
        zu, zl, yu, yl = masked_shifts(v, grid_masks, 1, 2)
        s = x_up(v) + x_down(v) + (zu + zl) + (yu + yl)
        return v + a * (s - 6.0 * v)

    def steps(ref, times):
        def one(k, carry):
            ref[...] = substep(ref[...])
            return carry

        lax.fori_loop(0, 2 * times, one, 0)

    for k in range(1, n):
        mc_copy(k, lax.rem(me + n - k, n)).wait_recv()

    @pl.when(me < C)
    def _():
        gather_wait_recv(gs, csw, css, csr)
        steps(csw, 1)

    p_x.wait()
    smooth(pb, pa, 1, H + 1)
    smooth(pb, pa, H + X - 1, X + 2 * H - 1)
    leftover(pa, 0, HC)
    leftover(pa, HC + Xc - 2, W)
    coarse_correct(pa)
    smooth(pa, pc, H - 1, H + X + 1)

    def finish(i):
        v = pc[i]
        zu, zl, yu, yl = masked_shifts(v, fine_masks, 0, 1)
        k = i - H + 1
        half = 0.5 * m[i]
        out[0, i - H] = pr[0, k] - half * (zu - zl)
        out[1, i - H] = pr[1, k] - half * (pc[i + 1] - pc[i - 1])
        out[2, i - H] = pr[2, k] - half * (yu - yl)

    planes(H, H + X, finish)
    for d in range(C):
        fill(0, Xc, lambda j: out[d, 2 * j] + out[d, 2 * j + 1], d * Xc)
    ce[...] = averaged(C * Xc).reshape(C, Xc, Zc, Yc)
    gather_start(ce, cew, ces, cer)

    def final_copy(d, peer):
        return pltpu.make_async_remote_copy(
            part.at[len(spans), pl.ds(peer * Xc, Xc)], wfin.at[d], fs.at[peer], fr.at[d],
            device_id={"space": peer}, device_id_type=MESH)

    @pl.when(me < C)
    def _():
        gather_wait_recv(ce, cew, ces, cer)
        part[0] = jnp.where(tm == 0, cew[...], cew[...] - csw[...])
        for r, s in enumerate(spans):
            def hop(target):
                return pltpu.make_async_remote_copy(
                    part.at[r], recv.at[r], ss.at[r], sr.at[r], device_id={"tm": target}, device_id_type=MESH)

            @pl.when(tm + s < ntm)
            def _():
                hop(tm + s).start()

            @pl.when(tm >= s)
            def _():
                hop(tm).wait_recv()
                steps(recv.at[r], s)
                part[r + 1] = part[r] + recv[r]

            @pl.when(tm < s)
            def _():
                part[r + 1] = part[r]

        for peer in range(n):
            @pl.when(me != peer)
            def _():
                final_copy(me, peer).start()

            @pl.when(me == peer)
            def _():
                wfin[peer if peer < C else 0] = part[len(spans), pl.ds(peer * Xc, Xc)]

    for d in range(C):
        @pl.when(me != d)
        def _():
            final_copy(d, d).wait_recv()

    prolonged((wfin[...] - ce[...]).reshape(C * Xc, Zc, Yc))
    for d in range(C):
        def add(j):
            c = rs[rows_at(d * Xc + j, Z), :]
            for h in range(2):
                out[d, 2 * j + h] = out[d, 2 * j + h] + c

        planes(0, Xc, add, 4)

    for k in range(1, n):
        mc_copy(k, me).wait_send()
    gather_wait_send(gs, csw, css, csr)
    gather_wait_send(ce, cew, ces, cer)

    @pl.when(me < C)
    def _():
        for r, s in enumerate(spans):
            @pl.when(tm + s < ntm)
            def _():
                pltpu.make_async_remote_copy(
                    part.at[r], recv.at[r], ss.at[r], sr.at[r],
                    device_id={"tm": tm + s}, device_id_type=MESH).wait_send()
        for peer in range(n):
            @pl.when(me != peer)
            def _():
                final_copy(me, peer).wait_send()


def body(n, ntm, start_states, labels):
    C, Z, X, Y = start_states.shape[1:]
    Xc, Zc, Yc = X // 2, Z // 2, Y // 2
    HC = H // 2
    spans = []
    while (1 << len(spans)) < ntm:
        spans.append(1 << len(spans))
    wide = pltpu.VMEM((X + 2 * H, Z, Y), f32)
    W = Xc + 2 * HC - 2
    grid = pltpu.VMEM((n * Xc, Zc, Yc), f32)
    rows = max(W, Xc + 2, C * Xc) * Z
    R = len(spans)
    dma = pltpu.SemaphoreType.DMA
    scratch = [
        pltpu.VMEM((C, Z, X, Y), f32), pltpu.VMEM((Z, X, Y), jnp.int32),
        pltpu.VMEM((C, X + 4, Z, Y), f32), wide, pltpu.VMEM((C, X + 2, Z, Y), f32),
        wide, wide, wide, wide, wide, wide, wide, wide, wide, wide, wide,
        pltpu.VMEM((rows, Y), f32), pltpu.VMEM((rows, Yc), f32),
        pltpu.VMEM((Xc + 2 * HC, Zc, Yc), f32), pltpu.VMEM((7, W, Zc, Yc), f32),
        pltpu.VMEM((C, Xc, Zc, Yc), f32), grid, grid, grid, pltpu.VMEM((C, Xc, Zc, Yc), f32),
        pltpu.VMEM((R + 1, n * Xc, Zc, Yc), f32), pltpu.VMEM((max(R, 1), n * Xc, Zc, Yc), f32),
        pltpu.VMEM((C, Xc, Zc, Yc), f32),
        pltpu.VMEM((Y, Yc), jnp.bfloat16), pltpu.VMEM((Yc, Y), jnp.bfloat16),
        dma((2,)), dma((2, C)), dma((2, C)), dma((2, 1)), dma((2, 1)), dma((2, 1)), dma((2, 1)),
        dma((2, 1)), dma((2, 1)), dma((n,)), dma((n,)), dma((C,)), dma((n,)), dma((C,)), dma((n,)),
        dma((max(R, 1),)), dma((max(R, 1),)), dma((n,)), dma((C,)),
    ]
    result = pl.pallas_call(
        functools.partial(kernel, n, ntm, spans),
        out_shape=jax.ShapeDtypeStruct((C, X, Z, Y), f32),
        in_specs=[pl.BlockSpec(memory_space=pl.ANY)] * 2,
        out_specs=pl.BlockSpec(memory_space=pltpu.VMEM),
        scratch_shapes=scratch,
        compiler_params=pltpu.CompilerParams(
            collective_id=0, has_side_effects=True, vmem_limit_bytes=40 * 1024 * 1024),
    )(start_states[0], labels)
    return jnp.swapaxes(result, 1, 2)[None]


def solution(mesh):
    in_specs = (P("tm", None, None, "space", None), P(None, "space", None))
    out_specs = P("tm", None, None, "space", None)
    fn = functools.partial(body, mesh.shape["space"], mesh.shape["tm"])
    return jax.shard_map(fn, mesh=mesh, in_specs=in_specs, out_specs=out_specs, check_vma=False)
```

```python
import functools
import jax
import jax.numpy as jnp
from jax import lax
from jax.experimental import pallas as pl
from jax.experimental.pallas import tpu as pltpu
from jax.sharding import PartitionSpec as P

VISCOSITY = 0.1
BUOYANCY = 0.2
OMEGA = 0.8
RATE = 0.15
CYCLES = 2
SWEEPS = 4
H = 10
MESH = pl.DeviceIdType.MESH
f32 = jnp.float32


def split_dot(a, b):
    a1 = a.astype(jnp.bfloat16)
    rest = a - a1.astype(f32)
    a2 = rest.astype(jnp.bfloat16)
    a3 = (rest - a2.astype(f32)).astype(jnp.bfloat16)
    dot = functools.partial(jnp.dot, preferred_element_type=f32)
    return dot(a1, b) + (dot(a2, b) + dot(a3, b))


def shifts(v, zaxis, yaxis):
    nz, ny = v.shape[zaxis], v.shape[yaxis]
    return (
        pltpu.roll(v, nz - 1, zaxis),
        pltpu.roll(v, 1, zaxis),
        pltpu.roll(v, ny - 1, yaxis),
        pltpu.roll(v, 1, yaxis),
    )


def edge_masks(shape, zaxis, yaxis):
    z = lax.broadcasted_iota(jnp.int32, shape, zaxis)
    y = lax.broadcasted_iota(jnp.int32, shape, yaxis)
    return z < shape[zaxis] - 1, z > 0, y < shape[yaxis] - 1, y > 0


def masked_shifts(v, masks, zaxis, yaxis):
    return [jnp.where(m, s, 0.0) for m, s in zip(masks, shifts(v, zaxis, yaxis))]


def planes(lo, hi, fn, step=8):
    def some(k, carry):
        for j in range(step):
            fn(lo + k * step + j)
        return carry

    turns = (hi - lo) // step
    if turns > 1:
        lax.fori_loop(0, turns, some, 0)
        lo = lo + turns * step
    for i in range(lo, hi):
        fn(i)


def rows_at(j, size):
    return pl.ds(j * size if isinstance(j, int) else pl.multiple_of(j * size, size), size)


def x_up(v):
    return jnp.concatenate([v[1:], jnp.zeros_like(v[:1])], axis=0)


def x_down(v):
    return jnp.concatenate([jnp.zeros_like(v[:1]), v[:-1]], axis=0)


def kernel(n, ntm, spans, u_in, l_in, out, u_raw, l_raw, u, m, pr, t, pa, pb, pc, rd, dg, wx, wzu, wzl, wyu, wyl,
           rs, rz, mc, cw, ce, mcw, csw, part, vb, down, dup,
           local_sem, us, ur, ms, mr, ts, tr, ps, pr_sem, mcs, mcr, css, csr, ss, sr, fs, fr):
    me, tm = lax.axis_index("space"), lax.axis_index("tm")
    Z, X, Y = u_in.shape[1:]
    Xc, Zc, Yc = X // 2, Z // 2, Y // 2
    HC = H // 2
    C = u_in.shape[0]
    hm = (vb.shape[2] - Xc) // 2
    R = len(spans)
    has_left, has_right = me > 0, me < n - 1

    loads = [
        pltpu.make_async_copy(u_in, u_raw, local_sem.at[0]),
        pltpu.make_async_copy(l_in, l_raw, local_sem.at[1]),
    ]
    for c in loads:
        c.start()

    barrier = pltpu.get_barrier_semaphore()
    count = jnp.where(has_left, 1, 0) + jnp.where(has_right, 1, 0)

    @pl.when(has_left)
    def _():
        pl.semaphore_signal(barrier, inc=1, device_id={"space": me - 1}, device_id_type=MESH)

    @pl.when(has_right)
    def _():
        pl.semaphore_signal(barrier, inc=1, device_id={"space": me + 1}, device_id_type=MESH)

    for s in spans:
        @pl.when(tm >= s)
        def _():
            pl.semaphore_signal(barrier, inc=1, device_id={"tm": tm - s}, device_id_type=MESH)

        @pl.when(tm + s < ntm)
        def _():
            pl.semaphore_signal(barrier, inc=1, device_id={"tm": tm + s}, device_id_type=MESH)

        count = count + jnp.where(tm >= s, 1, 0) + jnp.where(tm + s < ntm, 1, 0)

    @pl.when(jnp.logical_not(has_left))
    def _():
        u[:, 0:2] = jnp.zeros((C, 2, Z, Y), f32)
        for ref in (m, t, pb):
            ref[0:H] = jnp.zeros((H, Z, Y), f32)
        mcw[0:hm] = jnp.zeros((hm, Zc, Yc), f32)
        csw[:, 0:2] = jnp.zeros((C, 2, Zc, Yc), f32)
        vb[:, :, 0:hm] = jnp.zeros(vb.shape[:2] + (hm, Zc, Yc), f32)

    @pl.when(jnp.logical_not(has_right))
    def _():
        u[:, X + 2:X + 4] = jnp.zeros((C, 2, Z, Y), f32)
        for ref in (m, t, pb):
            ref[X + H:X + 2 * H] = jnp.zeros((H, Z, Y), f32)
        mcw[hm + Xc:] = jnp.zeros((hm, Zc, Yc), f32)
        csw[:, 2 + Xc:] = jnp.zeros((C, 2, Zc, Yc), f32)
        vb[:, :, hm + Xc:] = jnp.zeros(vb.shape[:2] + (hm, Zc, Yc), f32)

    row = lax.broadcasted_iota(jnp.int32, (Y, Yc), 0)
    col = lax.broadcasted_iota(jnp.int32, (Y, Yc), 1)
    down[...] = jnp.where(lax.div(row, 2) == col, 0.125, 0.0).astype(jnp.bfloat16)
    row = lax.broadcasted_iota(jnp.int32, (Yc, Y), 0)
    col = lax.broadcasted_iota(jnp.int32, (Yc, Y), 1)
    dup[...] = jnp.where(row == lax.div(col, 2), 1.0, 0.0).astype(jnp.bfloat16)

    def fill(lo, hi, plane_sum, base=0):
        def one(j):
            rs[rows_at(base + j, Z), :] = plane_sum(j)

        planes(lo, hi, one, 4)

    def restricted(count_c, plane_sum):
        fill(0, count_c, plane_sum)
        return averaged(count_c)

    def averaged(count_c):
        rows = count_c * Z
        rz[0:rows, :] = split_dot(rs[0:rows, :], down[...])
        half = rows // 2
        return (rz[pl.ds(0, half, stride=2), :] + rz[pl.ds(1, half, stride=2), :]).reshape(count_c, Zc, Yc)

    def prolonged(v):
        half = v.shape[0] * Zc
        flat = v.reshape(half, Yc)
        rz[pl.ds(0, half, stride=2), :] = flat
        rz[pl.ds(1, half, stride=2), :] = flat
        rs[0:2 * half, :] = split_dot(rz[0:2 * half, :], dup[...])

    def to_left(src, dst, ssem, rsem):
        return pltpu.make_async_remote_copy(src, dst, ssem, rsem, device_id={"space": me - 1}, device_id_type=MESH)

    def to_right(src, dst, ssem, rsem):
        return pltpu.make_async_remote_copy(src, dst, ssem, rsem, device_id={"space": me + 1}, device_id_type=MESH)

    class Exchange:
        def __init__(self, items, ssem, rsem, X=X):
            self.left, self.right = [], []
            for k, (at, first, width) in enumerate(items):
                self.left.append(to_left(at(first, width), at(first + X, width), ssem.at[0, k], rsem.at[0, k]))
                self.right.append(
                    to_right(at(first + X - width, width), at(first - width, width), ssem.at[1, k], rsem.at[1, k]))

        def start(self):
            @pl.when(has_left)
            def _():
                for c in self.left:
                    c.start()

            @pl.when(has_right)
            def _():
                for c in self.right:
                    c.start()

        def wait(self):
            @pl.when(has_left)
            def _():
                for c in self.left:
                    c.wait_send()
                for c in self.right:
                    c.wait_recv()

            @pl.when(has_right)
            def _():
                for c in self.right:
                    c.wait_send()
                for c in self.left:
                    c.wait_recv()

    def plane_view(ref):
        return lambda first, width: ref.at[pl.ds(first, width)]

    loads[0].wait()
    for d in range(C):
        u[d, 2:2 + X] = jnp.swapaxes(u_raw[d], 0, 1)
    loads[1].wait()
    m[H:H + X] = jnp.swapaxes(1.0 - 0.75 * l_raw[...].astype(f32), 0, 1)
    pl.semaphore_wait(barrier, count)

    u_x = Exchange([(lambda f, w, d=d: u.at[d, pl.ds(f, w)], 2, 2 if d == 1 else 1) for d in range(C)], us, ur)
    m_x = Exchange([(plane_view(m), H, H)], ms, mr)
    t_x = Exchange([(plane_view(t), H, H - 1)], ts, tr)
    p_x = Exchange([(plane_view(pb), H, H)], ps, pr_sem)
    u_x.start()
    m_x.start()

    mine = restricted(Xc, lambda j: m[H + 2 * j] + m[H + 2 * j + 1])
    mc[HC:HC + Xc] = mine
    mcw[hm:hm + Xc] = mine
    for d in range(C):
        fill(0, Xc, lambda j: u[d, 2 + 2 * j] + u[d, 3 + 2 * j], d * Xc)
    csw[:, 2:2 + Xc] = averaged(C * Xc).reshape(C, Xc, Zc, Yc)
    mc_x = Exchange([(plane_view(mcw), hm, hm)], mcs, mcr, Xc)
    cs_x = Exchange([(lambda f, w: csw.at[:, pl.ds(f, w)], 2, 2)], css, csr, Xc)

    fine_masks = edge_masks((Z, Y), 0, 1)

    def lap(d, i):
        v = u[d, i]
        summed = u[d, i - 1] + u[d, i + 1]
        zu, zl, yu, yl = masked_shifts(v, fine_masks, 0, 1)
        summed = summed + (zu + zl) + (yu + yl)
        return v + VISCOSITY * (summed - 6.0 * v)

    u_x.wait()

    def predict(i):
        pr[0, i] = lap(0, i + 1) + BUOYANCY * (2.0 * m[i - 1 + H] - 1.0)
        pr[1, i] = lap(1, i + 1)
        pr[2, i] = lap(2, i + 1)

    planes(1, X + 1, predict)
    pr[1, 0] = jnp.where(has_left, lap(1, 1), 0.0)
    pr[1, X + 1] = jnp.where(has_right, lap(1, X + 2), 0.0)

    def aim(i):
        zu, zl, _, _ = masked_shifts(pr[0, i], fine_masks, 0, 1)
        _, _, yu, yl = masked_shifts(pr[2, i], fine_masks, 0, 1)
        t[i - 1 + H] = -0.5 * ((zu - zl) + (pr[1, i + 1] - pr[1, i - 1]) + (yu - yl))

    planes(1, X + 1, aim)
    t_x.start()

    m_x.wait()

    def weigh(i):
        v = m[i]
        up, low = 0.5 * (v + m[i + 1]), 0.5 * (v + m[i - 1])
        wx[i] = up
        total = up + low
        for ref, mask, s in zip((wzu, wzl, wyu, wyl), fine_masks, shifts(v, 0, 1)):
            total = total + 0.5 * (v + jnp.where(mask, s, 0.0))
            ref[i] = jnp.where(mask, 0.5 * (v + s), 0.0)
        dg[i] = total
        rd[i] = jnp.where(v > 0.0, OMEGA / jnp.where(v > 0.0, total, 1.0), 0.0)

    wx[0] = 0.5 * (m[0] + m[1])
    planes(1, X + 2 * H - 1, weigh)

    mc[0:HC] = restricted(HC, lambda j: m[2 * j] + m[2 * j + 1])
    mc[HC + Xc:] = restricted(HC, lambda j: m[H + X + 2 * j] + m[H + X + 2 * j + 1])
    W = Xc + 2 * HC - 2
    mid = mc[1:1 + W]
    coarse_masks = edge_masks((W, Zc, Yc), 1, 2)
    cw[0] = 0.125 * (mid + mc[2:2 + W])
    cw[1] = 0.125 * (mid + mc[0:W])
    total = cw[0] + cw[1]
    for k, (mask, s) in enumerate(zip(coarse_masks, shifts(mid, 1, 2))):
        total = total + 0.125 * (mid + jnp.where(mask, s, 0.0))
        cw[2 + k] = jnp.where(mask, 0.125 * (mid + s), 0.0)
    cw[6] = jnp.where(mid > 0.0, OMEGA / jnp.where(mid > 0.0, total, 1.0), 0.0)

    def flux(p, i):
        v = p[i]
        zu, zl, yu, yl = shifts(v, 0, 1)
        s = wx[i] * p[i + 1] + wx[i - 1] * p[i - 1]
        s = s + (wzu[i] * zu + wzl[i] * zl)
        return v, s + (wyu[i] * yu + wyl[i] * yl)

    def smooth(src, dst, lo, hi):
        def one(i):
            v, s = flux(src, i)
            dst[i] = (1.0 - OMEGA) * v + rd[i] * (t[i] + s)

        planes(lo, hi, one)

    def residual(p, i):
        v, s = flux(p, i)
        return t[i] - dg[i] * v + s

    first = H - 2 * (HC - 1)

    def leftover(p, lo, hi):
        fill(lo, hi, lambda j: residual(p, first + 2 * j) + residual(p, first + 2 * j + 1))

    def coarse_correct(p):
        left = averaged(W)
        v = cw[6] * left
        for _ in range(SWEEPS - 1):
            zu, zl, yu, yl = shifts(v, 1, 2)
            s = cw[0] * x_up(v) + cw[1] * x_down(v) + (cw[2] * zu + cw[3] * zl) + (cw[4] * yu + cw[5] * yl)
            v = (1.0 - OMEGA) * v + cw[6] * (left + s)
        prolonged(v[HC - 2:W - (HC - 2)])

        def add(j):
            c = rs[rows_at(j, Z), :]
            for h in range(2):
                p[H - 2 + 2 * j + h] = p[H - 2 + 2 * j + h] + c

        planes(0, Xc + 2, add, 5)

    t_x.wait()
    mc_x.start()
    cs_x.start()

    def first_guess(i):
        pa[i] = rd[i] * t[i]

    planes(1, X + 2 * H - 1, first_guess)
    leftover(pa, 0, W)
    coarse_correct(pa)
    smooth(pa, pb, H, H + X)
    p_x.start()

    smooth(pb, pa, H + 1, H + X - 1)
    leftover(pa, HC, HC + Xc - 2)
    def coarse_steps(v, times):
        for _ in range(2 * times):
            length = v.shape[0] - 2
            off = (Xc + 2 * hm - length) // 2
            mid = v[1:-1]
            zu, zl, yu, yl = masked_shifts(mid, edge_masks(mid.shape, 1, 2), 1, 2)
            s = v[2:] + v[:-2] + (zu + zl) + (yu + yl)
            v = mid + (RATE * mcw[off:off + length]) * (s - 6.0 * mid)
        return v

    mc_x.wait()
    cs_x.wait()
    for d in range(C):
        part[0, d] = jnp.where(tm == 0, 0.0, coarse_steps(csw[d], 1))
    p_x.wait()
    smooth(pb, pa, 1, H + 1)
    smooth(pb, pa, H + X - 1, X + 2 * H - 1)
    leftover(pa, 0, HC)
    leftover(pa, HC + Xc - 2, W)
    coarse_correct(pa)
    smooth(pa, pc, H - 1, H + X + 1)

    def finish(i):
        v = pc[i]
        zu, zl, yu, yl = masked_shifts(v, fine_masks, 0, 1)
        k = i - H + 1
        half = 0.5 * m[i]
        out[0, i - H] = pr[0, k] - half * (zu - zl)
        out[1, i - H] = pr[1, k] - half * (pc[i + 1] - pc[i - 1])
        out[2, i - H] = pr[2, k] - half * (yu - yl)

    planes(H, H + X, finish)
    for d in range(C):
        fill(0, Xc, lambda j: out[d, 2 * j] + out[d, 2 * j + 1], d * Xc)
    ce[...] = averaged(C * Xc).reshape(C, Xc, Zc, Yc)

    stages, starts = [], []
    for s in spans:
        starts.append(sum(stages))
        stages.append(max(1, -(-2 * s // Xc)))

    def hop(r, d, target):
        return pltpu.make_async_remote_copy(
            part.at[r, d], vb.at[starts[r], d, pl.ds(hm, Xc)], ss.at[r, d], sr.at[r, d],
            device_id={"tm": target}, device_id_type=MESH)

    def send(r, d):
        if r < R:
            @pl.when(tm + spans[r] < ntm)
            def _():
                hop(r, d, tm + spans[r]).start()

    def sides(r, q, d):
        k = starts[r] + q
        return Exchange([(lambda f, w: vb.at[k, d, pl.ds(f, w)], hm, 2 * spans[r] // stages[r])],
                        fs.at[k, d], fr.at[k, d], Xc)

    def advance(r, d):
        times = spans[r] // stages[r]
        for q in range(stages[r]):
            sides(r, q, d).wait()
            v = coarse_steps(vb[starts[r] + q, d, hm - 2 * times:hm + Xc + 2 * times], times)
            if q + 1 < stages[r]:
                vb[starts[r] + q + 1, d, hm:hm + Xc] = v
                sides(r, q + 1, d).start()
        part[r + 1, d] = part[r, d] + v
        send(r + 1, d)

    for d in range(C):
        part[0, d] = ce[d] - part[0, d]
        send(0, d)
    for r, s in enumerate(spans):
        @pl.when(tm < s)
        def _():
            for d in range(C):
                part[r + 1, d] = part[r, d]
                send(r + 1, d)

        @pl.when(tm >= s)
        def _():
            for d in range(C):
                hop(r, d, tm).wait_recv()
                sides(r, 0, d).start()
                if d > 0:
                    advance(r, d - 1)
            advance(r, C - 1)

    prolonged((part[R] - ce[...]).reshape(C * Xc, Zc, Yc))
    for d in range(C):
        def add(j):
            c = rs[rows_at(d * Xc + j, Z), :]
            for h in range(2):
                out[d, 2 * j + h] = out[d, 2 * j + h] + c

        planes(0, Xc, add, 4)

    for r, s in enumerate(spans):
        @pl.when(tm + s < ntm)
        def _():
            for d in range(C):
                hop(r, d, tm + s).wait_send()


def body(n, ntm, start_states, labels):
    C, Z, X, Y = start_states.shape[1:]
    Xc, Zc, Yc = X // 2, Z // 2, Y // 2
    HC = H // 2
    spans = []
    while (1 << len(spans)) < ntm:
        spans.append(1 << len(spans))
    wide = pltpu.VMEM((X + 2 * H, Z, Y), f32)
    W = Xc + 2 * HC - 2
    hm = min(2 * max(spans + [1]), Xc)
    total = sum(max(1, -(-2 * s // Xc)) for s in spans) or 1
    rows = max(W, Xc + 2, C * Xc) * Z
    R = len(spans)
    dma = pltpu.SemaphoreType.DMA
    scratch = [
        pltpu.VMEM((C, Z, X, Y), f32), pltpu.VMEM((Z, X, Y), jnp.int32),
        pltpu.VMEM((C, X + 4, Z, Y), f32), wide, pltpu.VMEM((C, X + 2, Z, Y), f32),
        wide, wide, wide, wide, wide, wide, wide, wide, wide, wide, wide,
        pltpu.VMEM((rows, Y), f32), pltpu.VMEM((rows, Yc), f32),
        pltpu.VMEM((Xc + 2 * HC, Zc, Yc), f32), pltpu.VMEM((7, W, Zc, Yc), f32),
        pltpu.VMEM((C, Xc, Zc, Yc), f32), pltpu.VMEM((Xc + 2 * hm, Zc, Yc), f32),
        pltpu.VMEM((C, Xc + 4, Zc, Yc), f32), pltpu.VMEM((R + 1, C, Xc, Zc, Yc), f32),
        pltpu.VMEM((total, C, Xc + 2 * hm, Zc, Yc), f32),
        pltpu.VMEM((Y, Yc), jnp.bfloat16), pltpu.VMEM((Yc, Y), jnp.bfloat16),
        dma((2,)), dma((2, C)), dma((2, C)), dma((2, 1)), dma((2, 1)), dma((2, 1)), dma((2, 1)),
        dma((2, 1)), dma((2, 1)), dma((2, 1)), dma((2, 1)), dma((2, 1)), dma((2, 1)),
        dma((max(R, 1), C)), dma((max(R, 1), C)), dma((total, C, 2, 1)), dma((total, C, 2, 1)),
    ]
    result = pl.pallas_call(
        functools.partial(kernel, n, ntm, spans),
        out_shape=jax.ShapeDtypeStruct((C, X, Z, Y), f32),
        in_specs=[pl.BlockSpec(memory_space=pltpu.HBM)] * 2,
        out_specs=pl.BlockSpec(memory_space=pltpu.VMEM),
        scratch_shapes=scratch,
        compiler_params=pltpu.CompilerParams(
            collective_id=0, has_side_effects=True, vmem_limit_bytes=60 * 1024 * 1024),
    )(start_states[0], labels)
    return jnp.swapaxes(result, 1, 2)[None]


def solution(mesh):
    in_specs = (P("tm", None, None, "space", None), P(None, "space", None))
    out_specs = P("tm", None, None, "space", None)
    fn = functools.partial(body, mesh.shape["space"], mesh.shape["tm"])
    return jax.shard_map(fn, mesh=mesh, in_specs=in_specs, out_specs=out_specs, check_vma=False)
```

```python
import functools
import jax
import jax.numpy as jnp
from jax import lax
from jax.experimental import pallas as pl
from jax.experimental.pallas import tpu as pltpu
from jax.sharding import PartitionSpec as P

VISCOSITY = 0.1
BUOYANCY = 0.2
OMEGA = 0.8
RATE = 0.15
CYCLES = 2
SWEEPS = 4
H = 3
HL = SWEEPS
MESH = pl.DeviceIdType.MESH
f32 = jnp.float32


def split_dot(a, b):
    a1 = a.astype(jnp.bfloat16)
    rest = a - a1.astype(f32)
    a2 = rest.astype(jnp.bfloat16)
    a3 = (rest - a2.astype(f32)).astype(jnp.bfloat16)
    dot = functools.partial(jnp.dot, preferred_element_type=f32)
    return dot(a1, b) + (dot(a2, b) + dot(a3, b))


def shifts(v, zaxis, yaxis):
    nz, ny = v.shape[zaxis], v.shape[yaxis]
    return (
        pltpu.roll(v, nz - 1, zaxis),
        pltpu.roll(v, 1, zaxis),
        pltpu.roll(v, ny - 1, yaxis),
        pltpu.roll(v, 1, yaxis),
    )


def edge_masks(shape, zaxis, yaxis):
    z = lax.broadcasted_iota(jnp.int32, shape, zaxis)
    y = lax.broadcasted_iota(jnp.int32, shape, yaxis)
    return z < shape[zaxis] - 1, z > 0, y < shape[yaxis] - 1, y > 0


def masked_shifts(v, masks, zaxis, yaxis):
    return [jnp.where(m, s, 0.0) for m, s in zip(masks, shifts(v, zaxis, yaxis))]


def planes(lo, hi, fn, step=8):
    def some(k, carry):
        for j in range(step):
            fn(lo + k * step + j)
        return carry

    turns = (hi - lo) // step
    if turns > 1:
        lax.fori_loop(0, turns, some, 0)
        lo = lo + turns * step
    for i in range(lo, hi):
        fn(i)


def rows_at(j, size):
    return pl.ds(j * size if isinstance(j, int) else pl.multiple_of(j * size, size), size)


def x_up(v):
    return jnp.concatenate([v[1:], jnp.zeros_like(v[:1])], axis=0)


def x_down(v):
    return jnp.concatenate([jnp.zeros_like(v[:1]), v[:-1]], axis=0)


def kernel(n, ntm, spans, u_in, l_in, out, u_raw, l_raw, u, m, pr, t, pa, pb, pc, rd, dg, wx, wzu, wzl, wyu, wyl,
           rs, rz, fin, lw, cw, ce, mcw, csw, part, vb, down, dup,
           local_sem, us, ur, ms, mr, ts, tr, ps, pr_sem, mcs, mcr, css, csr, ls, lr, ss, sr, fs, fr):
    me, tm = lax.axis_index("space"), lax.axis_index("tm")
    Z, X, Y = u_in.shape[1:]
    Xc, Zc, Yc = X // 2, Z // 2, Y // 2
    C = u_in.shape[0]
    hm = (vb.shape[2] - Xc) // 2
    R = len(spans)
    has_left, has_right = me > 0, me < n - 1

    loads = [
        pltpu.make_async_copy(u_in, u_raw, local_sem.at[0]),
        pltpu.make_async_copy(l_in, l_raw, local_sem.at[1]),
    ]
    for c in loads:
        c.start()

    barrier = pltpu.get_barrier_semaphore()
    count = jnp.where(has_left, 1, 0) + jnp.where(has_right, 1, 0)

    @pl.when(has_left)
    def _():
        pl.semaphore_signal(barrier, inc=1, device_id={"space": me - 1}, device_id_type=MESH)

    @pl.when(has_right)
    def _():
        pl.semaphore_signal(barrier, inc=1, device_id={"space": me + 1}, device_id_type=MESH)

    for s in spans:
        @pl.when(tm >= s)
        def _():
            pl.semaphore_signal(barrier, inc=1, device_id={"tm": tm - s}, device_id_type=MESH)

        @pl.when(tm + s < ntm)
        def _():
            pl.semaphore_signal(barrier, inc=1, device_id={"tm": tm + s}, device_id_type=MESH)

        count = count + jnp.where(tm >= s, 1, 0) + jnp.where(tm + s < ntm, 1, 0)

    @pl.when(jnp.logical_not(has_left))
    def _():
        u[:, 0:2] = jnp.zeros((C, 2, Z, Y), f32)
        for ref in (m, t, pb):
            ref[0:H] = jnp.zeros((H, Z, Y), f32)
        lw[:, 0:HL] = jnp.zeros((CYCLES, HL, Zc, Yc), f32)
        mcw[0:hm] = jnp.zeros((hm, Zc, Yc), f32)
        csw[:, 0:2] = jnp.zeros((C, 2, Zc, Yc), f32)
        vb[:, :, 0:hm] = jnp.zeros(vb.shape[:2] + (hm, Zc, Yc), f32)

    @pl.when(jnp.logical_not(has_right))
    def _():
        u[:, X + 2:X + 4] = jnp.zeros((C, 2, Z, Y), f32)
        for ref in (m, t, pb):
            ref[X + H:X + 2 * H] = jnp.zeros((H, Z, Y), f32)
        lw[:, HL + Xc:] = jnp.zeros((CYCLES, HL, Zc, Yc), f32)
        mcw[hm + Xc:] = jnp.zeros((hm, Zc, Yc), f32)
        csw[:, 2 + Xc:] = jnp.zeros((C, 2, Zc, Yc), f32)
        vb[:, :, hm + Xc:] = jnp.zeros(vb.shape[:2] + (hm, Zc, Yc), f32)

    row = lax.broadcasted_iota(jnp.int32, (Y, Yc), 0)
    col = lax.broadcasted_iota(jnp.int32, (Y, Yc), 1)
    down[...] = jnp.where(lax.div(row, 2) == col, 0.125, 0.0).astype(jnp.bfloat16)
    row = lax.broadcasted_iota(jnp.int32, (Yc, Y), 0)
    col = lax.broadcasted_iota(jnp.int32, (Yc, Y), 1)
    dup[...] = jnp.where(row == lax.div(col, 2), 1.0, 0.0).astype(jnp.bfloat16)

    def fill(lo, hi, plane_sum, base=0):
        def one(j):
            rs[rows_at(base + j, Z), :] = plane_sum(j)

        planes(lo, hi, one, 4)

    def restricted(count_c, plane_sum):
        fill(0, count_c, plane_sum)
        return averaged(count_c)

    def averaged(count_c):
        rows = count_c * Z
        rz[0:rows, :] = split_dot(rs[0:rows, :], down[...])
        half = rows // 2
        return (rz[pl.ds(0, half, stride=2), :] + rz[pl.ds(1, half, stride=2), :]).reshape(count_c, Zc, Yc)

    def prolonged(v):
        half = v.shape[0] * Zc
        flat = v.reshape(half, Yc)
        rz[pl.ds(0, half, stride=2), :] = flat
        rz[pl.ds(1, half, stride=2), :] = flat
        rs[0:2 * half, :] = split_dot(rz[0:2 * half, :], dup[...])

    def to_left(src, dst, ssem, rsem):
        return pltpu.make_async_remote_copy(src, dst, ssem, rsem, device_id={"space": me - 1}, device_id_type=MESH)

    def to_right(src, dst, ssem, rsem):
        return pltpu.make_async_remote_copy(src, dst, ssem, rsem, device_id={"space": me + 1}, device_id_type=MESH)

    class Exchange:
        def __init__(self, items, ssem, rsem, X=X):
            self.left, self.right = [], []
            for k, (at, first, width) in enumerate(items):
                self.left.append(to_left(at(first, width), at(first + X, width), ssem.at[0, k], rsem.at[0, k]))
                self.right.append(
                    to_right(at(first + X - width, width), at(first - width, width), ssem.at[1, k], rsem.at[1, k]))

        def start(self):
            @pl.when(has_left)
            def _():
                for c in self.left:
                    c.start()

            @pl.when(has_right)
            def _():
                for c in self.right:
                    c.start()

        def wait(self):
            @pl.when(has_left)
            def _():
                for c in self.left:
                    c.wait_send()
                for c in self.right:
                    c.wait_recv()

            @pl.when(has_right)
            def _():
                for c in self.right:
                    c.wait_send()
                for c in self.left:
                    c.wait_recv()

    def plane_view(ref):
        return lambda first, width: ref.at[pl.ds(first, width)]

    loads[0].wait()
    for d in range(C):
        u[d, 2:2 + X] = jnp.swapaxes(u_raw[d], 0, 1)
    loads[1].wait()
    m[H:H + X] = jnp.swapaxes(1.0 - 0.75 * l_raw[...].astype(f32), 0, 1)
    pl.semaphore_wait(barrier, count)

    u_x = Exchange([(lambda f, w, d=d: u.at[d, pl.ds(f, w)], 2, 2 if d == 1 else 1) for d in range(C)], us, ur)
    m_x = Exchange([(plane_view(m), H, H)], ms, mr)
    t_x = Exchange([(plane_view(t), H, H - 1)], ts, tr)
    l_x = [Exchange([(lambda f, w, k=k: lw.at[k, pl.ds(f, w)], HL, HL)], ls.at[k], lr.at[k], Xc) for k in range(CYCLES)]
    p_x = Exchange([(plane_view(pb), H, H)], ps, pr_sem)
    u_x.start()
    m_x.start()

    mine = restricted(Xc, lambda j: m[H + 2 * j] + m[H + 2 * j + 1])
    mcw[hm:hm + Xc] = mine
    for d in range(C):
        fill(0, Xc, lambda j: u[d, 2 + 2 * j] + u[d, 3 + 2 * j], d * Xc)
    csw[:, 2:2 + Xc] = averaged(C * Xc).reshape(C, Xc, Zc, Yc)
    mc_x = Exchange([(plane_view(mcw), hm, hm)], mcs, mcr, Xc)
    cs_x = Exchange([(lambda f, w: csw.at[:, pl.ds(f, w)], 2, 2)], css, csr, Xc)
    mc_x.start()

    fine_masks = edge_masks((Z, Y), 0, 1)

    def lap(d, i):
        v = u[d, i]
        summed = u[d, i - 1] + u[d, i + 1]
        zu, zl, yu, yl = masked_shifts(v, fine_masks, 0, 1)
        summed = summed + (zu + zl) + (yu + yl)
        return v + VISCOSITY * (summed - 6.0 * v)

    u_x.wait()

    def predict(i):
        pr[0, i] = lap(0, i + 1) + BUOYANCY * (2.0 * m[i - 1 + H] - 1.0)
        pr[1, i] = lap(1, i + 1)
        pr[2, i] = lap(2, i + 1)

    planes(1, X + 1, predict)
    pr[1, 0] = jnp.where(has_left, lap(1, 1), 0.0)
    pr[1, X + 1] = jnp.where(has_right, lap(1, X + 2), 0.0)

    def aim(i):
        zu, zl, _, _ = masked_shifts(pr[0, i], fine_masks, 0, 1)
        _, _, yu, yl = masked_shifts(pr[2, i], fine_masks, 0, 1)
        t[i - 1 + H] = -0.5 * ((zu - zl) + (pr[1, i + 1] - pr[1, i - 1]) + (yu - yl))

    planes(1, X + 1, aim)
    t_x.start()
    cs_x.start()

    m_x.wait()

    def weigh(i):
        v = m[i]
        up, low = 0.5 * (v + m[i + 1]), 0.5 * (v + m[i - 1])
        wx[i] = up
        total = up + low
        for ref, mask, s in zip((wzu, wzl, wyu, wyl), fine_masks, shifts(v, 0, 1)):
            total = total + 0.5 * (v + jnp.where(mask, s, 0.0))
            ref[i] = jnp.where(mask, 0.5 * (v + s), 0.0)
        dg[i] = total
        rd[i] = jnp.where(v > 0.0, OMEGA / jnp.where(v > 0.0, total, 1.0), 0.0)

    wx[0] = 0.5 * (m[0] + m[1])
    planes(1, X + 2 * H - 1, weigh)

    W = Xc + 2 * HL
    mc_x.wait()
    at = hm - HL
    mid = mcw[at:at + W]
    coarse_masks = edge_masks((W, Zc, Yc), 1, 2)
    cw[0] = 0.125 * (mid + mcw[at + 1:at + 1 + W])
    cw[1] = 0.125 * (mid + mcw[at - 1:at - 1 + W])
    total = cw[0] + cw[1]
    for k, (mask, s) in enumerate(zip(coarse_masks, shifts(mid, 1, 2))):
        total = total + 0.125 * (mid + jnp.where(mask, s, 0.0))
        cw[2 + k] = jnp.where(mask, 0.125 * (mid + s), 0.0)
    cw[6] = jnp.where(mid > 0.0, OMEGA / jnp.where(mid > 0.0, total, 1.0), 0.0)

    def flux(p, i):
        v = p[i]
        zu, zl, yu, yl = shifts(v, 0, 1)
        s = wx[i] * p[i + 1] + wx[i - 1] * p[i - 1]
        s = s + (wzu[i] * zu + wzl[i] * zl)
        return v, s + (wyu[i] * yu + wyl[i] * yl)

    def smooth(src, dst, lo, hi):
        def one(i):
            v, s = flux(src, i)
            dst[i] = (1.0 - OMEGA) * v + rd[i] * (t[i] + s)

        planes(lo, hi, one)

    def residual(p, i):
        v, s = flux(p, i)
        return t[i] - dg[i] * v + s

    def leftover(p, lo, hi):
        fill(lo, hi, lambda j: residual(p, H + 2 * j) + residual(p, H + 2 * j + 1))

    def coarse_correct(p, cycle, meanwhile):
        lw[cycle, HL:HL + Xc] = averaged(Xc)
        l_x[cycle].start()
        meanwhile()
        l_x[cycle].wait()
        left = lw[cycle]
        v = cw[6] * left
        for _ in range(SWEEPS - 1):
            zu, zl, yu, yl = shifts(v, 1, 2)
            s = cw[0] * x_up(v) + cw[1] * x_down(v) + (cw[2] * zu + cw[3] * zl) + (cw[4] * yu + cw[5] * yl)
            v = (1.0 - OMEGA) * v + cw[6] * (left + s)
        prolonged(v[HL - 1:W - (HL - 1)])

        def add(j):
            c = rs[rows_at(j, Z), :]
            for h in range(2):
                p[H - 2 + 2 * j + h] = p[H - 2 + 2 * j + h] + c

        planes(0, Xc + 2, add, 5)

    t_x.wait()

    def first_guess(i):
        pa[i] = rd[i] * t[i]

    planes(1, X + 2 * H - 1, first_guess)
    leftover(pa, 0, Xc)

    def coarse_steps(v, times):
        for _ in range(2 * times):
            length = v.shape[0] - 2
            off = (Xc + 2 * hm - length) // 2
            mid = v[1:-1]
            zu, zl, yu, yl = masked_shifts(mid, edge_masks(mid.shape, 1, 2), 1, 2)
            s = v[2:] + v[:-2] + (zu + zl) + (yu + yl)
            v = mid + (RATE * mcw[off:off + length]) * (s - 6.0 * mid)
        return v

    def step_starts():
        cs_x.wait()
        for d in range(C):
            part[0, d] = jnp.where(tm == 0, 0.0, coarse_steps(csw[d], 1))

    coarse_correct(pa, 0, step_starts)
    smooth(pa, pb, H, H + X)
    p_x.start()

    smooth(pb, pa, H + 1, H + X - 1)
    leftover(pa, 1, Xc - 1)

    p_x.wait()
    smooth(pb, pa, 1, H + 1)
    smooth(pb, pa, H + X - 1, X + 2 * H - 1)
    leftover(pa, 0, 1)
    leftover(pa, Xc - 1, Xc)
    coarse_correct(pa, 1, lambda: None)
    smooth(pa, pc, H - 1, H + X + 1)

    def finish(i):
        v = pc[i]
        zu, zl, yu, yl = masked_shifts(v, fine_masks, 0, 1)
        k = i - H + 1
        half = 0.5 * m[i]
        fin[0, i - H] = pr[0, k] - half * (zu - zl)
        fin[1, i - H] = pr[1, k] - half * (pc[i + 1] - pc[i - 1])
        fin[2, i - H] = pr[2, k] - half * (yu - yl)

    planes(H, H + X, finish)
    for d in range(C):
        fill(0, Xc, lambda j: fin[d, 2 * j] + fin[d, 2 * j + 1], d * Xc)
    ce[...] = averaged(C * Xc).reshape(C, Xc, Zc, Yc)

    stages, starts = [], []
    for s in spans:
        starts.append(sum(stages))
        stages.append(max(1, -(-2 * s // Xc)))

    def hop(r, d, target):
        return pltpu.make_async_remote_copy(
            part.at[r, d], vb.at[starts[r], d, pl.ds(hm, Xc)], ss.at[r, d], sr.at[r, d],
            device_id={"tm": target}, device_id_type=MESH)

    def send(r, d):
        if r < R:
            @pl.when(tm + spans[r] < ntm)
            def _():
                hop(r, d, tm + spans[r]).start()

    def sides(r, q, d):
        k = starts[r] + q
        return Exchange([(lambda f, w: vb.at[k, d, pl.ds(f, w)], hm, 2 * spans[r] // stages[r])],
                        fs.at[k, d], fr.at[k, d], Xc)

    def advance(r, d):
        times = spans[r] // stages[r]
        for q in range(stages[r]):
            sides(r, q, d).wait()
            v = coarse_steps(vb[starts[r] + q, d, hm - 2 * times:hm + Xc + 2 * times], times)
            if q + 1 < stages[r]:
                vb[starts[r] + q + 1, d, hm:hm + Xc] = v
                sides(r, q + 1, d).start()
        part[r + 1, d] = part[r, d] + v
        send(r + 1, d)

    for d in range(C):
        part[0, d] = ce[d] - part[0, d]
        send(0, d)
    for r, s in enumerate(spans):
        @pl.when(tm < s)
        def _():
            for d in range(C):
                part[r + 1, d] = part[r, d]
                send(r + 1, d)

        @pl.when(tm >= s)
        def _():
            for d in range(C):
                hop(r, d, tm).wait_recv()
                sides(r, 0, d).start()
                if d > 0:
                    advance(r, d - 1)
            advance(r, C - 1)

    prolonged((part[R] - ce[...]).reshape(C * Xc, Zc, Yc))
    for d in range(C):
        def add(j):
            c = rs[rows_at(d * Xc + j, Z), :]
            for h in range(2):
                fin[d, 2 * j + h] = fin[d, 2 * j + h] + c

        planes(0, Xc, add, 4)
        out[d] = jnp.swapaxes(fin[d], 0, 1)

    for r, s in enumerate(spans):
        @pl.when(tm + s < ntm)
        def _():
            for d in range(C):
                hop(r, d, tm + s).wait_send()


def body(n, ntm, start_states, labels):
    C, Z, X, Y = start_states.shape[1:]
    Xc, Zc, Yc = X // 2, Z // 2, Y // 2
    spans = []
    while (1 << len(spans)) < ntm:
        spans.append(1 << len(spans))
    wide = pltpu.VMEM((X + 2 * H, Z, Y), f32)
    W = Xc + 2 * HL
    hm = max(HL + 1, min(2 * max(spans + [1]), Xc))
    total = sum(max(1, -(-2 * s // Xc)) for s in spans) or 1
    rows = max(Xc + 2, C * Xc) * Z
    R = len(spans)
    dma = pltpu.SemaphoreType.DMA
    scratch = [
        pltpu.VMEM((C, Z, X, Y), f32), pltpu.VMEM((Z, X, Y), jnp.int32),
        pltpu.VMEM((C, X + 4, Z, Y), f32), wide, pltpu.VMEM((C, X + 2, Z, Y), f32),
        wide, wide, wide, wide, wide, wide, wide, wide, wide, wide, wide,
        pltpu.VMEM((rows, Y), f32), pltpu.VMEM((rows, Yc), f32),
        pltpu.VMEM((C, X, Z, Y), f32), pltpu.VMEM((CYCLES, W, Zc, Yc), f32), pltpu.VMEM((7, W, Zc, Yc), f32),
        pltpu.VMEM((C, Xc, Zc, Yc), f32), pltpu.VMEM((Xc + 2 * hm, Zc, Yc), f32),
        pltpu.VMEM((C, Xc + 4, Zc, Yc), f32), pltpu.VMEM((R + 1, C, Xc, Zc, Yc), f32),
        pltpu.VMEM((total, C, Xc + 2 * hm, Zc, Yc), f32),
        pltpu.VMEM((Y, Yc), jnp.bfloat16), pltpu.VMEM((Yc, Y), jnp.bfloat16),
        dma((2,)), dma((2, C)), dma((2, C)), dma((2, 1)), dma((2, 1)), dma((2, 1)), dma((2, 1)),
        dma((2, 1)), dma((2, 1)), dma((2, 1)), dma((2, 1)), dma((2, 1)), dma((2, 1)),
        dma((CYCLES, 2, 1)), dma((CYCLES, 2, 1)),
        dma((max(R, 1), C)), dma((max(R, 1), C)), dma((total, C, 2, 1)), dma((total, C, 2, 1)),
    ]
    result = pl.pallas_call(
        functools.partial(kernel, n, ntm, spans),
        out_shape=jax.ShapeDtypeStruct((C, Z, X, Y), f32),
        in_specs=[pl.BlockSpec(memory_space=pltpu.HBM)] * 2,
        out_specs=pl.BlockSpec(memory_space=pltpu.VMEM),
        scratch_shapes=scratch,
        compiler_params=pltpu.CompilerParams(
            collective_id=0, has_side_effects=True, vmem_limit_bytes=60 * 1024 * 1024),
    )(start_states[0], labels)
    return result[None]


def solution(mesh):
    in_specs = (P("tm", None, None, "space", None), P(None, "space", None))
    out_specs = P("tm", None, None, "space", None)
    fn = functools.partial(body, mesh.shape["space"], mesh.shape["tm"])
    return jax.shard_map(fn, mesh=mesh, in_specs=in_specs, out_specs=out_specs, check_vma=False)
```

```python
import functools
import jax
import jax.numpy as jnp
from jax import lax
from jax.experimental import pallas as pl
from jax.experimental.pallas import tpu as pltpu
from jax.sharding import PartitionSpec as P

VISCOSITY = 0.1
BUOYANCY = 0.2
OMEGA = 0.8
RATE = 0.15
CYCLES = 2
SWEEPS = 4
H = 10
MESH = pl.DeviceIdType.MESH
f32 = jnp.float32


def split_dot(a, b):
    a1 = a.astype(jnp.bfloat16)
    rest = a - a1.astype(f32)
    a2 = rest.astype(jnp.bfloat16)
    a3 = (rest - a2.astype(f32)).astype(jnp.bfloat16)
    dot = functools.partial(jnp.dot, preferred_element_type=f32)
    return dot(a1, b) + (dot(a2, b) + dot(a3, b))


def shifts(v, zaxis, yaxis):
    nz, ny = v.shape[zaxis], v.shape[yaxis]
    return (
        pltpu.roll(v, nz - 1, zaxis),
        pltpu.roll(v, 1, zaxis),
        pltpu.roll(v, ny - 1, yaxis),
        pltpu.roll(v, 1, yaxis),
    )


def edge_masks(shape, zaxis, yaxis):
    z = lax.broadcasted_iota(jnp.int32, shape, zaxis)
    y = lax.broadcasted_iota(jnp.int32, shape, yaxis)
    return z < shape[zaxis] - 1, z > 0, y < shape[yaxis] - 1, y > 0


def masked_shifts(v, masks, zaxis, yaxis):
    return [jnp.where(m, s, 0.0) for m, s in zip(masks, shifts(v, zaxis, yaxis))]


def planes(lo, hi, fn, step=8):
    def some(k, carry):
        for j in range(step):
            fn(lo + k * step + j)
        return carry

    turns = (hi - lo) // step
    if turns > 1:
        lax.fori_loop(0, turns, some, 0)
        lo = lo + turns * step
    for i in range(lo, hi):
        fn(i)


def rows_at(j, size):
    return pl.ds(j * size if isinstance(j, int) else pl.multiple_of(j * size, size), size)


def x_up(v):
    return jnp.concatenate([v[1:], jnp.zeros_like(v[:1])], axis=0)


def x_down(v):
    return jnp.concatenate([jnp.zeros_like(v[:1]), v[:-1]], axis=0)


def kernel(n, ntm, spans, u_in, l_in, out, u_raw, l_raw, u, m, pr, t, pa, pb, pc, rd, dg, wx, wzu, wzl, wyu, wyl,
           rs, rz, mc, cw, ce, mcw, csw, part, vb, down, dup,
           local_sem, us, ur, ms, mr, ts, tr, ps, pr_sem, mcs, mcr, css, csr, ss, sr, fs, fr, hs, hr):
    me, tm = lax.axis_index("space"), lax.axis_index("tm")
    Z, X, Y = u_in.shape[1:]
    Xc, Zc, Yc = X // 2, Z // 2, Y // 2
    HC = H // 2
    C = u_in.shape[0]
    hm = (vb.shape[2] - Xc) // 2
    R = len(spans)
    has_left, has_right = me > 0, me < n - 1

    loads = [
        pltpu.make_async_copy(u_in, u_raw, local_sem.at[0]),
        pltpu.make_async_copy(l_in, l_raw, local_sem.at[1]),
    ]
    for c in loads:
        c.start()

    barrier = pltpu.get_barrier_semaphore()
    count = jnp.where(has_left, 1, 0) + jnp.where(has_right, 1, 0)

    @pl.when(has_left)
    def _():
        pl.semaphore_signal(barrier, inc=1, device_id={"space": me - 1}, device_id_type=MESH)

    @pl.when(has_right)
    def _():
        pl.semaphore_signal(barrier, inc=1, device_id={"space": me + 1}, device_id_type=MESH)

    for s in spans:
        @pl.when(tm >= s)
        def _():
            pl.semaphore_signal(barrier, inc=1, device_id={"tm": tm - s}, device_id_type=MESH)

        @pl.when(tm + s < ntm)
        def _():
            pl.semaphore_signal(barrier, inc=1, device_id={"tm": tm + s}, device_id_type=MESH)

        count = count + jnp.where(tm >= s, 1, 0) + jnp.where(tm + s < ntm, 1, 0)
        if 4 * s <= Xc:
            for by, there in ((-s, tm >= s), (s, tm + s < ntm)):
                for side, beside in ((-1, has_left), (1, has_right)):
                    both = jnp.logical_and(there, beside)

                    @pl.when(both)
                    def _():
                        pl.semaphore_signal(
                            barrier, inc=1, device_id={"tm": tm + by, "space": me + side}, device_id_type=MESH)

                    count = count + jnp.where(both, 1, 0)

    @pl.when(jnp.logical_not(has_left))
    def _():
        u[:, 0:2] = jnp.zeros((C, 2, Z, Y), f32)
        for ref in (m, t, pb):
            ref[0:H] = jnp.zeros((H, Z, Y), f32)
        mcw[0:hm] = jnp.zeros((hm, Zc, Yc), f32)
        csw[:, 0:2] = jnp.zeros((C, 2, Zc, Yc), f32)
        vb[:, :, 0:hm] = jnp.zeros(vb.shape[:2] + (hm, Zc, Yc), f32)

    @pl.when(jnp.logical_not(has_right))
    def _():
        u[:, X + 2:X + 4] = jnp.zeros((C, 2, Z, Y), f32)
        for ref in (m, t, pb):
            ref[X + H:X + 2 * H] = jnp.zeros((H, Z, Y), f32)
        mcw[hm + Xc:] = jnp.zeros((hm, Zc, Yc), f32)
        csw[:, 2 + Xc:] = jnp.zeros((C, 2, Zc, Yc), f32)
        vb[:, :, hm + Xc:] = jnp.zeros(vb.shape[:2] + (hm, Zc, Yc), f32)

    row = lax.broadcasted_iota(jnp.int32, (Y, Yc), 0)
    col = lax.broadcasted_iota(jnp.int32, (Y, Yc), 1)
    down[...] = jnp.where(lax.div(row, 2) == col, 0.125, 0.0).astype(jnp.bfloat16)
    row = lax.broadcasted_iota(jnp.int32, (Yc, Y), 0)
    col = lax.broadcasted_iota(jnp.int32, (Yc, Y), 1)
    dup[...] = jnp.where(row == lax.div(col, 2), 1.0, 0.0).astype(jnp.bfloat16)

    def fill(lo, hi, plane_sum, base=0):
        def one(j):
            rs[rows_at(base + j, Z), :] = plane_sum(j)

        planes(lo, hi, one, 4)

    def restricted(count_c, plane_sum):
        fill(0, count_c, plane_sum)
        return averaged(count_c)

    def averaged(count_c):
        rows = count_c * Z
        rz[0:rows, :] = split_dot(rs[0:rows, :], down[...])
        half = rows // 2
        return (rz[pl.ds(0, half, stride=2), :] + rz[pl.ds(1, half, stride=2), :]).reshape(count_c, Zc, Yc)

    def prolonged(v):
        half = v.shape[0] * Zc
        flat = v.reshape(half, Yc)
        rz[pl.ds(0, half, stride=2), :] = flat
        rz[pl.ds(1, half, stride=2), :] = flat
        rs[0:2 * half, :] = split_dot(rz[0:2 * half, :], dup[...])

    def to_left(src, dst, ssem, rsem):
        return pltpu.make_async_remote_copy(src, dst, ssem, rsem, device_id={"space": me - 1}, device_id_type=MESH)

    def to_right(src, dst, ssem, rsem):
        return pltpu.make_async_remote_copy(src, dst, ssem, rsem, device_id={"space": me + 1}, device_id_type=MESH)

    class Exchange:
        def __init__(self, items, ssem, rsem, X=X):
            self.left, self.right = [], []
            for k, (at, first, width) in enumerate(items):
                self.left.append(to_left(at(first, width), at(first + X, width), ssem.at[0, k], rsem.at[0, k]))
                self.right.append(
                    to_right(at(first + X - width, width), at(first - width, width), ssem.at[1, k], rsem.at[1, k]))

        def start(self):
            @pl.when(has_left)
            def _():
                for c in self.left:
                    c.start()

            @pl.when(has_right)
            def _():
                for c in self.right:
                    c.start()

        def wait(self):
            @pl.when(has_left)
            def _():
                for c in self.left:
                    c.wait_send()
                for c in self.right:
                    c.wait_recv()

            @pl.when(has_right)
            def _():
                for c in self.right:
                    c.wait_send()
                for c in self.left:
                    c.wait_recv()

    def plane_view(ref):
        return lambda first, width: ref.at[pl.ds(first, width)]

    loads[0].wait()
    for d in range(C):
        u[d, 2:2 + X] = jnp.swapaxes(u_raw[d], 0, 1)
    loads[1].wait()
    m[H:H + X] = jnp.swapaxes(1.0 - 0.75 * l_raw[...].astype(f32), 0, 1)
    pl.semaphore_wait(barrier, count)

    u_x = Exchange([(lambda f, w, d=d: u.at[d, pl.ds(f, w)], 2, 2 if d == 1 else 1) for d in range(C)], us, ur)
    m_x = Exchange([(plane_view(m), H, H)], ms, mr)
    t_x = Exchange([(plane_view(t), H, H - 1)], ts, tr)
    p_x = Exchange([(plane_view(pb), H, H)], ps, pr_sem)
    u_x.start()
    m_x.start()

    mine = restricted(Xc, lambda j: m[H + 2 * j] + m[H + 2 * j + 1])
    mc[HC:HC + Xc] = mine
    mcw[hm:hm + Xc] = mine
    for d in range(C):
        fill(0, Xc, lambda j: u[d, 2 + 2 * j] + u[d, 3 + 2 * j], d * Xc)
    csw[:, 2:2 + Xc] = averaged(C * Xc).reshape(C, Xc, Zc, Yc)
    mc_x = Exchange([(plane_view(mcw), hm, hm)], mcs, mcr, Xc)
    cs_x = Exchange([(lambda f, w: csw.at[:, pl.ds(f, w)], 2, 2)], css, csr, Xc)

    fine_masks = edge_masks((Z, Y), 0, 1)

    def lap(d, i):
        v = u[d, i]
        summed = u[d, i - 1] + u[d, i + 1]
        zu, zl, yu, yl = masked_shifts(v, fine_masks, 0, 1)
        summed = summed + (zu + zl) + (yu + yl)
        return v + VISCOSITY * (summed - 6.0 * v)

    u_x.wait()

    def predict(i):
        pr[0, i] = lap(0, i + 1) + BUOYANCY * (2.0 * m[i - 1 + H] - 1.0)
        pr[1, i] = lap(1, i + 1)
        pr[2, i] = lap(2, i + 1)

    planes(1, X + 1, predict)
    pr[1, 0] = jnp.where(has_left, lap(1, 1), 0.0)
    pr[1, X + 1] = jnp.where(has_right, lap(1, X + 2), 0.0)

    def aim(i):
        zu, zl, _, _ = masked_shifts(pr[0, i], fine_masks, 0, 1)
        _, _, yu, yl = masked_shifts(pr[2, i], fine_masks, 0, 1)
        t[i - 1 + H] = -0.5 * ((zu - zl) + (pr[1, i + 1] - pr[1, i - 1]) + (yu - yl))

    planes(1, X + 1, aim)
    t_x.start()

    m_x.wait()

    def weigh(i):
        v = m[i]
        up, low = 0.5 * (v + m[i + 1]), 0.5 * (v + m[i - 1])
        wx[i] = up
        total = up + low
        for ref, mask, s in zip((wzu, wzl, wyu, wyl), fine_masks, shifts(v, 0, 1)):
            total = total + 0.5 * (v + jnp.where(mask, s, 0.0))
            ref[i] = jnp.where(mask, 0.5 * (v + s), 0.0)
        dg[i] = total
        rd[i] = jnp.where(v > 0.0, OMEGA / jnp.where(v > 0.0, total, 1.0), 0.0)

    wx[0] = 0.5 * (m[0] + m[1])
    planes(1, X + 2 * H - 1, weigh)

    mc[0:HC] = restricted(HC, lambda j: m[2 * j] + m[2 * j + 1])
    mc[HC + Xc:] = restricted(HC, lambda j: m[H + X + 2 * j] + m[H + X + 2 * j + 1])
    W = Xc + 2 * HC - 2
    mid = mc[1:1 + W]
    coarse_masks = edge_masks((W, Zc, Yc), 1, 2)
    cw[0] = 0.125 * (mid + mc[2:2 + W])
    cw[1] = 0.125 * (mid + mc[0:W])
    total = cw[0] + cw[1]
    for k, (mask, s) in enumerate(zip(coarse_masks, shifts(mid, 1, 2))):
        total = total + 0.125 * (mid + jnp.where(mask, s, 0.0))
        cw[2 + k] = jnp.where(mask, 0.125 * (mid + s), 0.0)
    cw[6] = jnp.where(mid > 0.0, OMEGA / jnp.where(mid > 0.0, total, 1.0), 0.0)

    def flux(p, i):
        v = p[i]
        zu, zl, yu, yl = shifts(v, 0, 1)
        s = wx[i] * p[i + 1] + wx[i - 1] * p[i - 1]
        s = s + (wzu[i] * zu + wzl[i] * zl)
        return v, s + (wyu[i] * yu + wyl[i] * yl)

    def smooth(src, dst, lo, hi):
        def one(i):
            v, s = flux(src, i)
            dst[i] = (1.0 - OMEGA) * v + rd[i] * (t[i] + s)

        planes(lo, hi, one)

    def residual(p, i):
        v, s = flux(p, i)
        return t[i] - dg[i] * v + s

    first = H - 2 * (HC - 1)

    def leftover(p, lo, hi):
        fill(lo, hi, lambda j: residual(p, first + 2 * j) + residual(p, first + 2 * j + 1))

    def coarse_correct(p):
        left = averaged(W)
        v = cw[6] * left
        for _ in range(SWEEPS - 1):
            zu, zl, yu, yl = shifts(v, 1, 2)
            s = cw[0] * x_up(v) + cw[1] * x_down(v) + (cw[2] * zu + cw[3] * zl) + (cw[4] * yu + cw[5] * yl)
            v = (1.0 - OMEGA) * v + cw[6] * (left + s)
        prolonged(v[HC - 2:W - (HC - 2)])

        def add(j):
            c = rs[rows_at(j, Z), :]
            for h in range(2):
                p[H - 2 + 2 * j + h] = p[H - 2 + 2 * j + h] + c

        planes(0, Xc + 2, add, 5)

    t_x.wait()
    mc_x.start()
    cs_x.start()

    def first_guess(i):
        pa[i] = rd[i] * t[i]

    planes(1, X + 2 * H - 1, first_guess)
    leftover(pa, 0, W)
    coarse_correct(pa)
    smooth(pa, pb, H, H + X)
    p_x.start()

    smooth(pb, pa, H + 1, H + X - 1)
    leftover(pa, HC, HC + Xc - 2)
    def coarse_steps(v, times):
        for _ in range(2 * times):
            length = v.shape[0] - 2
            off = (Xc + 2 * hm - length) // 2
            mid = v[1:-1]
            inner = [jnp.where(k, 1.0, 0.0) for k in edge_masks((1, Zc, Yc), 1, 2)]
            zu, zl, yu, yl = [a * b for a, b in zip(shifts(mid, 1, 2), inner)]
            s = v[2:] + v[:-2] + (zu + zl) + (yu + yl)
            v = mid + (RATE * mcw[off:off + length]) * (s - 6.0 * mid)
        return v

    mc_x.wait()
    cs_x.wait()
    for d in range(C):
        part[0, d] = jnp.where(tm == 0, 0.0, coarse_steps(csw[d], 1))
    p_x.wait()
    smooth(pb, pa, 1, H + 1)
    smooth(pb, pa, H + X - 1, X + 2 * H - 1)
    leftover(pa, 0, HC)
    leftover(pa, HC + Xc - 2, W)
    coarse_correct(pa)
    smooth(pa, pc, H - 1, H + X + 1)

    def finish(i):
        v = pc[i]
        zu, zl, yu, yl = masked_shifts(v, fine_masks, 0, 1)
        k = i - H + 1
        half = 0.5 * m[i]
        out[0, i - H] = pr[0, k] - half * (zu - zl)
        out[1, i - H] = pr[1, k] - half * (pc[i + 1] - pc[i - 1])
        out[2, i - H] = pr[2, k] - half * (yu - yl)

    planes(H, H + X, finish)
    for d in range(C):
        fill(0, Xc, lambda j: out[d, 2 * j] + out[d, 2 * j + 1], d * Xc)
    ce[...] = averaged(C * Xc).reshape(C, Xc, Zc, Yc)

    stages, starts = [], []
    for s in spans:
        starts.append(sum(stages))
        stages.append(max(1, -(-2 * s // Xc)))

    def hop(r, d, target):
        return pltpu.make_async_remote_copy(
            part.at[r, d], vb.at[starts[r], d, pl.ds(hm, Xc)], ss.at[r, d], sr.at[r, d],
            device_id={"tm": target}, device_id_type=MESH)

    def send(r, d):
        if r < R:
            @pl.when(tm + spans[r] < ntm)
            def _():
                hop(r, d, tm + spans[r]).start()

    def sides(r, q, d):
        k = starts[r] + q
        return Exchange([(lambda f, w: vb.at[k, d, pl.ds(f, w)], hm, 2 * spans[r] // stages[r])],
                        fs.at[k, d], fr.at[k, d], Xc)

    direct = [4 * s <= Xc for s in spans]

    def halo(r, side, target):
        h, k = 2 * spans[r], starts[r]
        src, dst = ((0, hm + Xc), (Xc - h, hm - h))[side]
        return pltpu.make_async_remote_copy(
            part.at[r, :, pl.ds(src, h)], vb.at[k, :, pl.ds(dst, h)], hs.at[r, side], hr.at[r, side],
            device_id={"tm": target, "space": me + (-1, 1)[side]}, device_id_type=MESH)

    def send_halo(r):
        if r < R and direct[r]:
            s = spans[r]
            for side, beside in enumerate((has_left, has_right)):
                @pl.when(jnp.logical_and(tm + s < ntm, beside))
                def _():
                    halo(r, side, tm + s).start()

    def advance(r, d):
        times = spans[r] // stages[r]
        for q in range(stages[r]):
            if not direct[r]:
                sides(r, q, d).wait()
            v = coarse_steps(vb[starts[r] + q, d, hm - 2 * times:hm + Xc + 2 * times], times)
            if q + 1 < stages[r]:
                vb[starts[r] + q + 1, d, hm:hm + Xc] = v
                sides(r, q + 1, d).start()
        part[r + 1, d] = part[r, d] + v
        send(r + 1, d)

    for d in range(C):
        part[0, d] = ce[d] - part[0, d]
        send(0, d)
    send_halo(0)
    for r, s in enumerate(spans):
        @pl.when(tm < s)
        def _():
            for d in range(C):
                part[r + 1, d] = part[r, d]
                send(r + 1, d)
            send_halo(r + 1)

        @pl.when(tm >= s)
        def _():
            if direct[r]:
                for side, beside in enumerate((has_right, has_left)):
                    @pl.when(beside)
                    def _():
                        halo(r, side, tm).wait_recv()

                for d in range(C):
                    hop(r, d, tm).wait_recv()
                    advance(r, d)
            else:
                for d in range(C):
                    hop(r, d, tm).wait_recv()
                    sides(r, 0, d).start()
                for d in range(C):
                    advance(r, d)
            send_halo(r + 1)

    prolonged((part[R] - ce[...]).reshape(C * Xc, Zc, Yc))
    for d in range(C):
        def add(j):
            c = rs[rows_at(d * Xc + j, Z), :]
            for h in range(2):
                out[d, 2 * j + h] = out[d, 2 * j + h] + c

        planes(0, Xc, add, 4)

    for r, s in enumerate(spans):
        @pl.when(tm + s < ntm)
        def _():
            for d in range(C):
                hop(r, d, tm + s).wait_send()
        if direct[r]:
            for side, beside in enumerate((has_left, has_right)):
                @pl.when(jnp.logical_and(tm + s < ntm, beside))
                def _():
                    halo(r, side, tm + s).wait_send()


def body(n, ntm, start_states, labels):
    C, Z, X, Y = start_states.shape[1:]
    Xc, Zc, Yc = X // 2, Z // 2, Y // 2
    HC = H // 2
    spans = []
    while (1 << len(spans)) < ntm:
        spans.append(1 << len(spans))
    wide = pltpu.VMEM((X + 2 * H, Z, Y), f32)
    W = Xc + 2 * HC - 2
    hm = min(2 * max(spans + [1]), Xc)
    total = sum(max(1, -(-2 * s // Xc)) for s in spans) or 1
    rows = max(W, Xc + 2, C * Xc) * Z
    R = len(spans)
    dma = pltpu.SemaphoreType.DMA
    scratch = [
        pltpu.VMEM((C, Z, X, Y), f32), pltpu.VMEM((Z, X, Y), jnp.int32),
        pltpu.VMEM((C, X + 4, Z, Y), f32), wide, pltpu.VMEM((C, X + 2, Z, Y), f32),
        wide, wide, wide, wide, wide, wide, wide, wide, wide, wide, wide,
        pltpu.VMEM((rows, Y), f32), pltpu.VMEM((rows, Yc), f32),
        pltpu.VMEM((Xc + 2 * HC, Zc, Yc), f32), pltpu.VMEM((7, W, Zc, Yc), f32),
        pltpu.VMEM((C, Xc, Zc, Yc), f32), pltpu.VMEM((Xc + 2 * hm, Zc, Yc), f32),
        pltpu.VMEM((C, Xc + 4, Zc, Yc), f32), pltpu.VMEM((R + 1, C, Xc, Zc, Yc), f32),
        pltpu.VMEM((total, C, Xc + 2 * hm, Zc, Yc), f32),
        pltpu.VMEM((Y, Yc), jnp.bfloat16), pltpu.VMEM((Yc, Y), jnp.bfloat16),
        dma((2,)), dma((2, C)), dma((2, C)), dma((2, 1)), dma((2, 1)), dma((2, 1)), dma((2, 1)),
        dma((2, 1)), dma((2, 1)), dma((2, 1)), dma((2, 1)), dma((2, 1)), dma((2, 1)),
        dma((max(R, 1), C)), dma((max(R, 1), C)), dma((total, C, 2, 1)), dma((total, C, 2, 1)),
        dma((max(R, 1), 2)), dma((max(R, 1), 2)),
    ]
    result = pl.pallas_call(
        functools.partial(kernel, n, ntm, spans),
        out_shape=jax.ShapeDtypeStruct((C, X, Z, Y), f32),
        in_specs=[pl.BlockSpec(memory_space=pltpu.HBM)] * 2,
        out_specs=pl.BlockSpec(memory_space=pltpu.VMEM),
        scratch_shapes=scratch,
        compiler_params=pltpu.CompilerParams(
            collective_id=0, has_side_effects=True, vmem_limit_bytes=60 * 1024 * 1024),
    )(start_states[0], labels)
    return jnp.swapaxes(result, 1, 2)[None]


def solution(mesh):
    in_specs = (P("tm", None, None, "space", None), P(None, "space", None))
    out_specs = P("tm", None, None, "space", None)
    fn = functools.partial(body, mesh.shape["space"], mesh.shape["tm"])
    return jax.shard_map(fn, mesh=mesh, in_specs=in_specs, out_specs=out_specs, check_vma=False)
```

```python
import functools
import jax
import jax.numpy as jnp
from jax import lax
from jax.experimental import pallas as pl
from jax.experimental.pallas import tpu as pltpu
from jax.sharding import PartitionSpec as P

VISCOSITY = 0.1
BUOYANCY = 0.2
OMEGA = 0.8
RATE = 0.15
CYCLES = 2
SWEEPS = 4
H = 10
MESH = pl.DeviceIdType.MESH
f32 = jnp.float32


def split_dot(a, b):
    a1 = a.astype(jnp.bfloat16)
    rest = a - a1.astype(f32)
    a2 = rest.astype(jnp.bfloat16)
    a3 = (rest - a2.astype(f32)).astype(jnp.bfloat16)
    dot = functools.partial(jnp.dot, preferred_element_type=f32)
    return dot(a1, b) + (dot(a2, b) + dot(a3, b))


def shifts(v, zaxis, yaxis):
    nz, ny = v.shape[zaxis], v.shape[yaxis]
    return (
        pltpu.roll(v, nz - 1, zaxis),
        pltpu.roll(v, 1, zaxis),
        pltpu.roll(v, ny - 1, yaxis),
        pltpu.roll(v, 1, yaxis),
    )


def edge_masks(shape, zaxis, yaxis):
    z = lax.broadcasted_iota(jnp.int32, shape, zaxis)
    y = lax.broadcasted_iota(jnp.int32, shape, yaxis)
    return z < shape[zaxis] - 1, z > 0, y < shape[yaxis] - 1, y > 0


def masked_shifts(v, masks, zaxis, yaxis):
    return [jnp.where(m, s, 0.0) for m, s in zip(masks, shifts(v, zaxis, yaxis))]


def planes(lo, hi, fn, step=8):
    def some(k, carry):
        for j in range(step):
            fn(lo + k * step + j)
        return carry

    turns = (hi - lo) // step
    if turns > 1:
        lax.fori_loop(0, turns, some, 0)
        lo = lo + turns * step
    for i in range(lo, hi):
        fn(i)


def rows_at(j, size):
    return pl.ds(j * size if isinstance(j, int) else pl.multiple_of(j * size, size), size)


def x_up(v):
    return jnp.concatenate([v[1:], jnp.zeros_like(v[:1])], axis=0)


def x_down(v):
    return jnp.concatenate([jnp.zeros_like(v[:1]), v[:-1]], axis=0)


def kernel(n, ntm, spans, u_in, l_in, out, u_raw, l_raw, u, m, pr, t, pa, pb, pc, rd, dg, wx, wzu, wzl, wyu, wyl,
           rs, rz, mc, cw, ce, mcw, csw, part, vb, down, dup,
           local_sem, us, ur, ms, mr, ts, tr, ps, pr_sem, mcs, mcr, css, csr, ss, sr, fs, fr, hs, hr):
    me, tm = lax.axis_index("space"), lax.axis_index("tm")
    Z, X, Y = u_in.shape[1:]
    Xc, Zc, Yc = X // 2, Z // 2, Y // 2
    HC = H // 2
    C = u_in.shape[0]
    hm = (vb.shape[2] - Xc) // 2
    R = len(spans)
    has_left, has_right = me > 0, me < n - 1

    loads = [
        pltpu.make_async_copy(u_in, u_raw, local_sem.at[0]),
        pltpu.make_async_copy(l_in, l_raw, local_sem.at[1]),
    ]
    for c in loads:
        c.start()

    barrier = pltpu.get_barrier_semaphore()
    count = jnp.where(has_left, 1, 0) + jnp.where(has_right, 1, 0)

    @pl.when(has_left)
    def _():
        pl.semaphore_signal(barrier, inc=1, device_id={"space": me - 1}, device_id_type=MESH)

    @pl.when(has_right)
    def _():
        pl.semaphore_signal(barrier, inc=1, device_id={"space": me + 1}, device_id_type=MESH)

    for s in spans:
        @pl.when(tm >= s)
        def _():
            pl.semaphore_signal(barrier, inc=1, device_id={"tm": tm - s}, device_id_type=MESH)

        @pl.when(tm + s < ntm)
        def _():
            pl.semaphore_signal(barrier, inc=1, device_id={"tm": tm + s}, device_id_type=MESH)

        count = count + jnp.where(tm >= s, 1, 0) + jnp.where(tm + s < ntm, 1, 0)
        if 4 * s <= Xc:
            for by, there in ((-s, tm >= s), (s, tm + s < ntm)):
                for side, beside in ((-1, has_left), (1, has_right)):
                    both = jnp.logical_and(there, beside)

                    @pl.when(both)
                    def _():
                        pl.semaphore_signal(
                            barrier, inc=1, device_id={"tm": tm + by, "space": me + side}, device_id_type=MESH)

                    count = count + jnp.where(both, 1, 0)

    @pl.when(jnp.logical_not(has_left))
    def _():
        u[:, 0:2] = jnp.zeros((C, 2, Z, Y), f32)
        for ref in (m, t, pb):
            ref[0:H] = jnp.zeros((H, Z, Y), f32)
        mcw[0:hm] = jnp.zeros((hm, Zc, Yc), f32)
        csw[:, 0:2] = jnp.zeros((C, 2, Zc, Yc), f32)
        vb[:, :, 0:hm] = jnp.zeros(vb.shape[:2] + (hm, Zc, Yc), f32)

    @pl.when(jnp.logical_not(has_right))
    def _():
        u[:, X + 2:X + 4] = jnp.zeros((C, 2, Z, Y), f32)
        for ref in (m, t, pb):
            ref[X + H:X + 2 * H] = jnp.zeros((H, Z, Y), f32)
        mcw[hm + Xc:] = jnp.zeros((hm, Zc, Yc), f32)
        csw[:, 2 + Xc:] = jnp.zeros((C, 2, Zc, Yc), f32)
        vb[:, :, hm + Xc:] = jnp.zeros(vb.shape[:2] + (hm, Zc, Yc), f32)

    row = lax.broadcasted_iota(jnp.int32, (Y, Yc), 0)
    col = lax.broadcasted_iota(jnp.int32, (Y, Yc), 1)
    down[...] = jnp.where(lax.div(row, 2) == col, 0.125, 0.0).astype(jnp.bfloat16)
    row = lax.broadcasted_iota(jnp.int32, (Yc, Y), 0)
    col = lax.broadcasted_iota(jnp.int32, (Yc, Y), 1)
    dup[...] = jnp.where(row == lax.div(col, 2), 1.0, 0.0).astype(jnp.bfloat16)

    def fill(lo, hi, plane_sum, base=0):
        def one(j):
            rs[rows_at(base + j, Z), :] = plane_sum(j)

        planes(lo, hi, one, 4)

    def restricted(count_c, plane_sum):
        fill(0, count_c, plane_sum)
        return averaged(count_c)

    def averaged(count_c):
        rows = count_c * Z
        rz[0:rows, :] = split_dot(rs[0:rows, :], down[...])
        half = rows // 2
        return (rz[pl.ds(0, half, stride=2), :] + rz[pl.ds(1, half, stride=2), :]).reshape(count_c, Zc, Yc)

    def prolonged(v):
        half = v.shape[0] * Zc
        flat = v.reshape(half, Yc)
        rz[pl.ds(0, half, stride=2), :] = flat
        rz[pl.ds(1, half, stride=2), :] = flat
        rs[0:2 * half, :] = split_dot(rz[0:2 * half, :], dup[...])

    def to_left(src, dst, ssem, rsem):
        return pltpu.make_async_remote_copy(src, dst, ssem, rsem, device_id={"space": me - 1}, device_id_type=MESH)

    def to_right(src, dst, ssem, rsem):
        return pltpu.make_async_remote_copy(src, dst, ssem, rsem, device_id={"space": me + 1}, device_id_type=MESH)

    class Exchange:
        def __init__(self, items, ssem, rsem, X=X):
            self.left, self.right = [], []
            for k, (at, first, width) in enumerate(items):
                self.left.append(to_left(at(first, width), at(first + X, width), ssem.at[0, k], rsem.at[0, k]))
                self.right.append(
                    to_right(at(first + X - width, width), at(first - width, width), ssem.at[1, k], rsem.at[1, k]))

        def start(self):
            @pl.when(has_left)
            def _():
                for c in self.left:
                    c.start()

            @pl.when(has_right)
            def _():
                for c in self.right:
                    c.start()

        def wait(self):
            @pl.when(has_left)
            def _():
                for c in self.left:
                    c.wait_send()
                for c in self.right:
                    c.wait_recv()

            @pl.when(has_right)
            def _():
                for c in self.right:
                    c.wait_send()
                for c in self.left:
                    c.wait_recv()

    def plane_view(ref):
        return lambda first, width: ref.at[pl.ds(first, width)]

    loads[0].wait()
    for d in range(C):
        u[d, 2:2 + X] = jnp.swapaxes(u_raw[d], 0, 1)
    loads[1].wait()
    m[H:H + X] = jnp.swapaxes(1.0 - 0.75 * l_raw[...].astype(f32), 0, 1)
    pl.semaphore_wait(barrier, count)

    u_x = Exchange([(lambda f, w, d=d: u.at[d, pl.ds(f, w)], 2, 2 if d == 1 else 1) for d in range(C)], us, ur)
    m_x = Exchange([(plane_view(m), H, H)], ms, mr)
    t_x = Exchange([(plane_view(t), H, H - 1)], ts, tr)
    p_x = Exchange([(plane_view(pb), H, H)], ps, pr_sem)
    u_x.start()
    m_x.start()

    fine_masks = edge_masks((Z, Y), 0, 1)

    def lap(d, i):
        v = u[d, i]
        summed = u[d, i - 1] + u[d, i + 1]
        zu, zl, yu, yl = masked_shifts(v, fine_masks, 0, 1)
        summed = summed + (zu + zl) + (yu + yl)
        return v + VISCOSITY * (summed - 6.0 * v)

    def predict(i):
        pr[0, i] = lap(0, i + 1) + BUOYANCY * (2.0 * m[i - 1 + H] - 1.0)
        pr[1, i] = lap(1, i + 1)
        pr[2, i] = lap(2, i + 1)

    planes(2, X, predict, 7)

    def aim(i):
        zu, zl, _, _ = masked_shifts(pr[0, i], fine_masks, 0, 1)
        _, _, yu, yl = masked_shifts(pr[2, i], fine_masks, 0, 1)
        t[i - 1 + H] = -0.5 * ((zu - zl) + (pr[1, i + 1] - pr[1, i - 1]) + (yu - yl))

    planes(3, X - 1, aim, 6)
    u_x.wait()
    predict(1)
    predict(X)
    pr[1, 0] = jnp.where(has_left, lap(1, 1), 0.0)
    pr[1, X + 1] = jnp.where(has_right, lap(1, X + 2), 0.0)

    for i in (1, 2, X - 1, X):
        aim(i)
    t_x.start()

    mine = restricted(Xc, lambda j: m[H + 2 * j] + m[H + 2 * j + 1])
    mc[HC:HC + Xc] = mine
    mcw[hm:hm + Xc] = mine
    for d in range(C):
        fill(0, Xc, lambda j: u[d, 2 + 2 * j] + u[d, 3 + 2 * j], d * Xc)
    csw[:, 2:2 + Xc] = averaged(C * Xc).reshape(C, Xc, Zc, Yc)
    mc_x = Exchange([(plane_view(mcw), hm, hm)], mcs, mcr, Xc)
    cs_x = Exchange([(lambda f, w: csw.at[:, pl.ds(f, w)], 2, 2)], css, csr, Xc)

    m_x.wait()

    def weigh(i):
        v = m[i]
        up, low = 0.5 * (v + m[i + 1]), 0.5 * (v + m[i - 1])
        wx[i] = up
        total = up + low
        for ref, mask, s in zip((wzu, wzl, wyu, wyl), fine_masks, shifts(v, 0, 1)):
            total = total + 0.5 * (v + jnp.where(mask, s, 0.0))
            ref[i] = jnp.where(mask, 0.5 * (v + s), 0.0)
        dg[i] = total
        rd[i] = jnp.where(v > 0.0, OMEGA / jnp.where(v > 0.0, total, 1.0), 0.0)

    wx[0] = 0.5 * (m[0] + m[1])
    planes(1, X + 2 * H - 1, weigh)

    mc[0:HC] = restricted(HC, lambda j: m[2 * j] + m[2 * j + 1])
    mc[HC + Xc:] = restricted(HC, lambda j: m[H + X + 2 * j] + m[H + X + 2 * j + 1])
    W = Xc + 2 * HC - 2
    mid = mc[1:1 + W]
    coarse_masks = edge_masks((W, Zc, Yc), 1, 2)
    cw[0] = 0.125 * (mid + mc[2:2 + W])
    cw[1] = 0.125 * (mid + mc[0:W])
    total = cw[0] + cw[1]
    for k, (mask, s) in enumerate(zip(coarse_masks, shifts(mid, 1, 2))):
        total = total + 0.125 * (mid + jnp.where(mask, s, 0.0))
        cw[2 + k] = jnp.where(mask, 0.125 * (mid + s), 0.0)
    cw[6] = jnp.where(mid > 0.0, OMEGA / jnp.where(mid > 0.0, total, 1.0), 0.0)

    def flux(p, i):
        v = p[i]
        zu, zl, yu, yl = shifts(v, 0, 1)
        s = wx[i] * p[i + 1] + wx[i - 1] * p[i - 1]
        s = s + (wzu[i] * zu + wzl[i] * zl)
        return v, s + (wyu[i] * yu + wyl[i] * yl)

    def smooth(src, dst, lo, hi):
        def one(i):
            v, s = flux(src, i)
            dst[i] = (1.0 - OMEGA) * v + rd[i] * (t[i] + s)

        planes(lo, hi, one)

    def residual(p, i):
        v, s = flux(p, i)
        return t[i] - dg[i] * v + s

    first = H - 2 * (HC - 1)

    def leftover(p, lo, hi):
        fill(lo, hi, lambda j: residual(p, first + 2 * j) + residual(p, first + 2 * j + 1))

    def coarse_correct(p):
        left = averaged(W)
        v = cw[6] * left
        for _ in range(SWEEPS - 1):
            zu, zl, yu, yl = shifts(v, 1, 2)
            s = cw[0] * x_up(v) + cw[1] * x_down(v) + (cw[2] * zu + cw[3] * zl) + (cw[4] * yu + cw[5] * yl)
            v = (1.0 - OMEGA) * v + cw[6] * (left + s)
        prolonged(v[HC - 2:W - (HC - 2)])

        def add(j):
            c = rs[rows_at(j, Z), :]
            for h in range(2):
                p[H - 2 + 2 * j + h] = p[H - 2 + 2 * j + h] + c

        planes(0, Xc + 2, add, 5)

    t_x.wait()
    mc_x.start()
    cs_x.start()

    def first_guess(i):
        pa[i] = rd[i] * t[i]

    planes(1, X + 2 * H - 1, first_guess)
    leftover(pa, 0, W)
    coarse_correct(pa)
    smooth(pa, pb, H, H + X)
    p_x.start()

    smooth(pb, pa, H + 1, H + X - 1)
    leftover(pa, HC, HC + Xc - 2)
    def coarse_steps(v, times):
        for _ in range(2 * times):
            length = v.shape[0] - 2
            off = (Xc + 2 * hm - length) // 2
            mid = v[1:-1]
            inner = [jnp.where(k, 1.0, 0.0) for k in edge_masks((1, Zc, Yc), 1, 2)]
            zu, zl, yu, yl = [a * b for a, b in zip(shifts(mid, 1, 2), inner)]
            s = v[2:] + v[:-2] + (zu + zl) + (yu + yl)
            v = mid + (RATE * mcw[off:off + length]) * (s - 6.0 * mid)
        return v

    mc_x.wait()
    cs_x.wait()
    for d in range(C):
        part[0, d] = jnp.where(tm == 0, 0.0, coarse_steps(csw[d], 1))
    p_x.wait()
    smooth(pb, pa, 1, H + 1)
    smooth(pb, pa, H + X - 1, X + 2 * H - 1)
    leftover(pa, 0, HC)
    leftover(pa, HC + Xc - 2, W)
    coarse_correct(pa)
    smooth(pa, pc, H - 1, H + X + 1)

    def finish(i):
        v = pc[i]
        zu, zl, yu, yl = masked_shifts(v, fine_masks, 0, 1)
        k = i - H + 1
        half = 0.5 * m[i]
        out[0, i - H] = pr[0, k] - half * (zu - zl)
        out[1, i - H] = pr[1, k] - half * (pc[i + 1] - pc[i - 1])
        out[2, i - H] = pr[2, k] - half * (yu - yl)

    planes(H, H + X, finish)
    for d in range(C):
        fill(0, Xc, lambda j: out[d, 2 * j] + out[d, 2 * j + 1], d * Xc)
    ce[...] = averaged(C * Xc).reshape(C, Xc, Zc, Yc)

    stages, starts = [], []
    for s in spans:
        starts.append(sum(stages))
        stages.append(max(1, -(-2 * s // Xc)))

    def hop(r, d, target):
        return pltpu.make_async_remote_copy(
            part.at[r, d], vb.at[starts[r], d, pl.ds(hm, Xc)], ss.at[r, d], sr.at[r, d],
            device_id={"tm": target}, device_id_type=MESH)

    def send(r, d):
        if r < R:
            @pl.when(tm + spans[r] < ntm)
            def _():
                hop(r, d, tm + spans[r]).start()

    def sides(r, q, d):
        k = starts[r] + q
        return Exchange([(lambda f, w: vb.at[k, d, pl.ds(f, w)], hm, 2 * spans[r] // stages[r])],
                        fs.at[k, d], fr.at[k, d], Xc)

    direct = [4 * s <= Xc for s in spans]

    def halo(r, side, target):
        h, k = 2 * spans[r], starts[r]
        src, dst = ((0, hm + Xc), (Xc - h, hm - h))[side]
        return pltpu.make_async_remote_copy(
            part.at[r, :, pl.ds(src, h)], vb.at[k, :, pl.ds(dst, h)], hs.at[r, side], hr.at[r, side],
            device_id={"tm": target, "space": me + (-1, 1)[side]}, device_id_type=MESH)

    def send_halo(r):
        if r < R and direct[r]:
            s = spans[r]
            for side, beside in enumerate((has_left, has_right)):
                @pl.when(jnp.logical_and(tm + s < ntm, beside))
                def _():
                    halo(r, side, tm + s).start()

    def advance(r, d):
        times = spans[r] // stages[r]
        for q in range(stages[r]):
            if not direct[r]:
                sides(r, q, d).wait()
            v = coarse_steps(vb[starts[r] + q, d, hm - 2 * times:hm + Xc + 2 * times], times)
            if q + 1 < stages[r]:
                vb[starts[r] + q + 1, d, hm:hm + Xc] = v
                sides(r, q + 1, d).start()
        part[r + 1, d] = part[r, d] + v
        send(r + 1, d)

    for d in range(C):
        part[0, d] = ce[d] - part[0, d]
        send(0, d)
    send_halo(0)
    for r, s in enumerate(spans):
        @pl.when(tm < s)
        def _():
            for d in range(C):
                part[r + 1, d] = part[r, d]
                send(r + 1, d)
            send_halo(r + 1)

        @pl.when(tm >= s)
        def _():
            if direct[r]:
                for side, beside in enumerate((has_right, has_left)):
                    @pl.when(beside)
                    def _():
                        halo(r, side, tm).wait_recv()

                for d in range(C):
                    hop(r, d, tm).wait_recv()
                    advance(r, d)
            else:
                for d in range(C):
                    hop(r, d, tm).wait_recv()
                    sides(r, 0, d).start()
                for d in range(C):
                    advance(r, d)
            send_halo(r + 1)

    prolonged((part[R] - ce[...]).reshape(C * Xc, Zc, Yc))
    for d in range(C):
        def add(j):
            c = rs[rows_at(d * Xc + j, Z), :]
            for h in range(2):
                out[d, 2 * j + h] = out[d, 2 * j + h] + c

        planes(0, Xc, add, 4)

    for r, s in enumerate(spans):
        @pl.when(tm + s < ntm)
        def _():
            for d in range(C):
                hop(r, d, tm + s).wait_send()
        if direct[r]:
            for side, beside in enumerate((has_left, has_right)):
                @pl.when(jnp.logical_and(tm + s < ntm, beside))
                def _():
                    halo(r, side, tm + s).wait_send()


def body(n, ntm, start_states, labels):
    C, Z, X, Y = start_states.shape[1:]
    Xc, Zc, Yc = X // 2, Z // 2, Y // 2
    HC = H // 2
    spans = []
    while (1 << len(spans)) < ntm:
        spans.append(1 << len(spans))
    wide = pltpu.VMEM((X + 2 * H, Z, Y), f32)
    W = Xc + 2 * HC - 2
    hm = min(2 * max(spans + [1]), Xc)
    total = sum(max(1, -(-2 * s // Xc)) for s in spans) or 1
    rows = max(W, Xc + 2, C * Xc) * Z
    R = len(spans)
    dma = pltpu.SemaphoreType.DMA
    scratch = [
        pltpu.VMEM((C, Z, X, Y), f32), pltpu.VMEM((Z, X, Y), jnp.int32),
        pltpu.VMEM((C, X + 4, Z, Y), f32), wide, pltpu.VMEM((C, X + 2, Z, Y), f32),
        wide, wide, wide, wide, wide, wide, wide, wide, wide, wide, wide,
        pltpu.VMEM((rows, Y), f32), pltpu.VMEM((rows, Yc), f32),
        pltpu.VMEM((Xc + 2 * HC, Zc, Yc), f32), pltpu.VMEM((7, W, Zc, Yc), f32),
        pltpu.VMEM((C, Xc, Zc, Yc), f32), pltpu.VMEM((Xc + 2 * hm, Zc, Yc), f32),
        pltpu.VMEM((C, Xc + 4, Zc, Yc), f32), pltpu.VMEM((R + 1, C, Xc, Zc, Yc), f32),
        pltpu.VMEM((total, C, Xc + 2 * hm, Zc, Yc), f32),
        pltpu.VMEM((Y, Yc), jnp.bfloat16), pltpu.VMEM((Yc, Y), jnp.bfloat16),
        dma((2,)), dma((2, C)), dma((2, C)), dma((2, 1)), dma((2, 1)), dma((2, 1)), dma((2, 1)),
        dma((2, 1)), dma((2, 1)), dma((2, 1)), dma((2, 1)), dma((2, 1)), dma((2, 1)),
        dma((max(R, 1), C)), dma((max(R, 1), C)), dma((total, C, 2, 1)), dma((total, C, 2, 1)),
        dma((max(R, 1), 2)), dma((max(R, 1), 2)),
    ]
    result = pl.pallas_call(
        functools.partial(kernel, n, ntm, spans),
        out_shape=jax.ShapeDtypeStruct((C, X, Z, Y), f32),
        in_specs=[pl.BlockSpec(memory_space=pltpu.HBM)] * 2,
        out_specs=pl.BlockSpec(memory_space=pltpu.VMEM),
        scratch_shapes=scratch,
        compiler_params=pltpu.CompilerParams(
            collective_id=0, has_side_effects=True, vmem_limit_bytes=60 * 1024 * 1024),
    )(start_states[0], labels)
    return jnp.swapaxes(result, 1, 2)[None]


def solution(mesh):
    in_specs = (P("tm", None, None, "space", None), P(None, "space", None))
    out_specs = P("tm", None, None, "space", None)
    fn = functools.partial(body, mesh.shape["space"], mesh.shape["tm"])
    return jax.shard_map(fn, mesh=mesh, in_specs=in_specs, out_specs=out_specs, check_vma=False)
```

```python
import functools
import jax
import jax.numpy as jnp
from jax import lax
from jax.experimental import pallas as pl
from jax.experimental.pallas import tpu as pltpu
from jax.sharding import PartitionSpec as P

VISCOSITY = 0.1
BUOYANCY = 0.2
OMEGA = 0.8
RATE = 0.15
CYCLES = 2
SWEEPS = 4
H = 10
MESH = pl.DeviceIdType.MESH
f32 = jnp.float32


def split_dot(a, b):
    a1 = a.astype(jnp.bfloat16)
    rest = a - a1.astype(f32)
    a2 = rest.astype(jnp.bfloat16)
    a3 = (rest - a2.astype(f32)).astype(jnp.bfloat16)
    dot = functools.partial(jnp.dot, preferred_element_type=f32)
    return dot(a1, b) + (dot(a2, b) + dot(a3, b))


def shifts(v, zaxis, yaxis):
    nz, ny = v.shape[zaxis], v.shape[yaxis]
    return (
        pltpu.roll(v, nz - 1, zaxis),
        pltpu.roll(v, 1, zaxis),
        pltpu.roll(v, ny - 1, yaxis),
        pltpu.roll(v, 1, yaxis),
    )


def edge_masks(shape, zaxis, yaxis):
    z = lax.broadcasted_iota(jnp.int32, shape, zaxis)
    y = lax.broadcasted_iota(jnp.int32, shape, yaxis)
    return z < shape[zaxis] - 1, z > 0, y < shape[yaxis] - 1, y > 0


def masked_shifts(v, masks, zaxis, yaxis):
    return [jnp.where(m, s, 0.0) for m, s in zip(masks, shifts(v, zaxis, yaxis))]


def planes(lo, hi, fn, step=8):
    def some(k, carry):
        for j in range(step):
            fn(lo + k * step + j)
        return carry

    turns = (hi - lo) // step
    if turns > 1:
        lax.fori_loop(0, turns, some, 0)
        lo = lo + turns * step
    for i in range(lo, hi):
        fn(i)


def rows_at(j, size):
    return pl.ds(j * size if isinstance(j, int) else pl.multiple_of(j * size, size), size)


def x_up(v):
    return jnp.concatenate([v[1:], jnp.zeros_like(v[:1])], axis=0)


def x_down(v):
    return jnp.concatenate([jnp.zeros_like(v[:1]), v[:-1]], axis=0)


def kernel(n, ntm, spans, u_in, l_in, out, u_raw, l_raw, u, m, pr, t, pa, pb, pc, rd, dg, wx, wzu, wzl, wyu, wyl,
           rs, rz, mc, cw, ce, mcw, csw, part, vb, down, dup,
           local_sem, us, ur, ms, mr, ts, tr, ps, pr_sem, mcs, mcr, css, csr, ss, sr, fs, fr, hs, hr):
    me, tm = lax.axis_index("space"), lax.axis_index("tm")
    Z, X, Y = u_in.shape[1:]
    Xc, Zc, Yc = X // 2, Z // 2, Y // 2
    HC = H // 2
    C = u_in.shape[0]
    hm = (vb.shape[2] - Xc) // 2
    R = len(spans)
    has_left, has_right = me > 0, me < n - 1

    loads = [
        pltpu.make_async_copy(u_in, u_raw, local_sem.at[0]),
        pltpu.make_async_copy(l_in, l_raw, local_sem.at[1]),
    ]
    for c in loads:
        c.start()

    barrier = pltpu.get_barrier_semaphore()
    count = jnp.where(has_left, 1, 0) + jnp.where(has_right, 1, 0)

    @pl.when(has_left)
    def _():
        pl.semaphore_signal(barrier, inc=1, device_id={"space": me - 1}, device_id_type=MESH)

    @pl.when(has_right)
    def _():
        pl.semaphore_signal(barrier, inc=1, device_id={"space": me + 1}, device_id_type=MESH)

    for s in spans:
        @pl.when(tm >= s)
        def _():
            pl.semaphore_signal(barrier, inc=1, device_id={"tm": tm - s}, device_id_type=MESH)

        @pl.when(tm + s < ntm)
        def _():
            pl.semaphore_signal(barrier, inc=1, device_id={"tm": tm + s}, device_id_type=MESH)

        count = count + jnp.where(tm >= s, 1, 0) + jnp.where(tm + s < ntm, 1, 0)
        if 4 * s <= Xc:
            for by, there in ((-s, tm >= s), (s, tm + s < ntm)):
                for side, beside in ((-1, has_left), (1, has_right)):
                    both = jnp.logical_and(there, beside)

                    @pl.when(both)
                    def _():
                        pl.semaphore_signal(
                            barrier, inc=1, device_id={"tm": tm + by, "space": me + side}, device_id_type=MESH)

                    count = count + jnp.where(both, 1, 0)

    @pl.when(jnp.logical_not(has_left))
    def _():
        u[:, 0:2] = jnp.zeros((C, 2, Z, Y), f32)
        for ref in (m, t, pb):
            ref[0:H] = jnp.zeros((H, Z, Y), f32)
        mcw[0:hm] = jnp.zeros((hm, Zc, Yc), f32)
        csw[:, 0:2] = jnp.zeros((C, 2, Zc, Yc), f32)
        vb[:, :, 0:hm] = jnp.zeros(vb.shape[:2] + (hm, Zc, Yc), f32)

    @pl.when(jnp.logical_not(has_right))
    def _():
        u[:, X + 2:X + 4] = jnp.zeros((C, 2, Z, Y), f32)
        for ref in (m, t, pb):
            ref[X + H:X + 2 * H] = jnp.zeros((H, Z, Y), f32)
        mcw[hm + Xc:] = jnp.zeros((hm, Zc, Yc), f32)
        csw[:, 2 + Xc:] = jnp.zeros((C, 2, Zc, Yc), f32)
        vb[:, :, hm + Xc:] = jnp.zeros(vb.shape[:2] + (hm, Zc, Yc), f32)

    row = lax.broadcasted_iota(jnp.int32, (Y, Yc), 0)
    col = lax.broadcasted_iota(jnp.int32, (Y, Yc), 1)
    down[...] = jnp.where(lax.div(row, 2) == col, 0.125, 0.0).astype(jnp.bfloat16)
    row = lax.broadcasted_iota(jnp.int32, (Yc, Y), 0)
    col = lax.broadcasted_iota(jnp.int32, (Yc, Y), 1)
    dup[...] = jnp.where(row == lax.div(col, 2), 1.0, 0.0).astype(jnp.bfloat16)

    def fill(lo, hi, plane_sum, base=0):
        def one(j):
            rs[rows_at(base + j, Z), :] = plane_sum(j)

        planes(lo, hi, one, 4)

    def restricted(count_c, plane_sum):
        fill(0, count_c, plane_sum)
        return averaged(count_c)

    def averaged(count_c):
        rows = count_c * Z
        rz[0:rows, :] = split_dot(rs[0:rows, :], down[...])
        half = rows // 2
        return (rz[pl.ds(0, half, stride=2), :] + rz[pl.ds(1, half, stride=2), :]).reshape(count_c, Zc, Yc)

    def prolonged(v):
        half = v.shape[0] * Zc
        flat = v.reshape(half, Yc)
        rz[pl.ds(0, half, stride=2), :] = flat
        rz[pl.ds(1, half, stride=2), :] = flat
        rs[0:2 * half, :] = split_dot(rz[0:2 * half, :], dup[...])

    def to_left(src, dst, ssem, rsem):
        return pltpu.make_async_remote_copy(src, dst, ssem, rsem, device_id={"space": me - 1}, device_id_type=MESH)

    def to_right(src, dst, ssem, rsem):
        return pltpu.make_async_remote_copy(src, dst, ssem, rsem, device_id={"space": me + 1}, device_id_type=MESH)

    class Exchange:
        def __init__(self, items, ssem, rsem, X=X):
            self.left, self.right = [], []
            for k, (at, first, width) in enumerate(items):
                self.left.append(to_left(at(first, width), at(first + X, width), ssem.at[0, k], rsem.at[0, k]))
                self.right.append(
                    to_right(at(first + X - width, width), at(first - width, width), ssem.at[1, k], rsem.at[1, k]))

        def start(self):
            @pl.when(has_left)
            def _():
                for c in self.left:
                    c.start()

            @pl.when(has_right)
            def _():
                for c in self.right:
                    c.start()

        def wait(self):
            @pl.when(has_left)
            def _():
                for c in self.left:
                    c.wait_send()
                for c in self.right:
                    c.wait_recv()

            @pl.when(has_right)
            def _():
                for c in self.right:
                    c.wait_send()
                for c in self.left:
                    c.wait_recv()

    def plane_view(ref):
        return lambda first, width: ref.at[pl.ds(first, width)]

    loads[0].wait()
    for d in range(C):
        u[d, 2:2 + X] = jnp.swapaxes(u_raw[d], 0, 1)
    loads[1].wait()
    m[H:H + X] = jnp.swapaxes(1.0 - 0.75 * l_raw[...].astype(f32), 0, 1)
    pl.semaphore_wait(barrier, count)

    u_x = Exchange([(lambda f, w, d=d: u.at[d, pl.ds(f, w)], 2, 2 if d == 1 else 1) for d in range(C)], us, ur)
    m_x = Exchange([(plane_view(m), H, H)], ms, mr)
    t_x = Exchange([(plane_view(t), H, H - 1)], ts, tr)
    p_x = Exchange([(plane_view(pb), H, H)], ps, pr_sem)
    u_x.start()
    m_x.start()

    fine_masks = edge_masks((Z, Y), 0, 1)

    def lap(d, i):
        v = u[d, i]
        summed = u[d, i - 1] + u[d, i + 1]
        zu, zl, yu, yl = masked_shifts(v, fine_masks, 0, 1)
        summed = summed + (zu + zl) + (yu + yl)
        return v + VISCOSITY * (summed - 6.0 * v)

    def predict(i):
        pr[0, i] = lap(0, i + 1) + BUOYANCY * (2.0 * m[i - 1 + H] - 1.0)
        pr[1, i] = lap(1, i + 1)
        pr[2, i] = lap(2, i + 1)

    planes(2, X, predict, 7)

    def aim(i):
        zu, zl, _, _ = masked_shifts(pr[0, i], fine_masks, 0, 1)
        _, _, yu, yl = masked_shifts(pr[2, i], fine_masks, 0, 1)
        t[i - 1 + H] = -0.5 * ((zu - zl) + (pr[1, i + 1] - pr[1, i - 1]) + (yu - yl))

    planes(3, X - 1, aim, 6)
    u_x.wait()
    predict(1)
    predict(X)
    pr[1, 0] = jnp.where(has_left, lap(1, 1), 0.0)
    pr[1, X + 1] = jnp.where(has_right, lap(1, X + 2), 0.0)

    for i in (1, 2, X - 1, X):
        aim(i)
    t_x.start()

    mine = restricted(Xc, lambda j: m[H + 2 * j] + m[H + 2 * j + 1])
    mc[HC:HC + Xc] = mine
    mcw[hm:hm + Xc] = mine
    for d in range(C):
        fill(0, Xc, lambda j: u[d, 2 + 2 * j] + u[d, 3 + 2 * j], d * Xc)
    csw[:, 2:2 + Xc] = averaged(C * Xc).reshape(C, Xc, Zc, Yc)
    mc_x = Exchange([(plane_view(mcw), hm, hm)], mcs, mcr, Xc)
    cs_x = Exchange([(lambda f, w: csw.at[:, pl.ds(f, w)], 2, 2)], css, csr, Xc)

    m_x.wait()

    def weigh(i):
        v = m[i]
        up, low = 0.5 * (v + m[i + 1]), 0.5 * (v + m[i - 1])
        wx[i] = up
        total = up + low
        for ref, mask, s in zip((wzu, wzl, wyu, wyl), fine_masks, shifts(v, 0, 1)):
            total = total + 0.5 * (v + jnp.where(mask, s, 0.0))
            ref[i] = jnp.where(mask, 0.5 * (v + s), 0.0)
        dg[i] = total
        rd[i] = jnp.where(v > 0.0, OMEGA / jnp.where(v > 0.0, total, 1.0), 0.0)

    wx[0] = 0.5 * (m[0] + m[1])
    planes(1, X + 2 * H - 1, weigh)

    mc[0:HC] = restricted(HC, lambda j: m[2 * j] + m[2 * j + 1])
    mc[HC + Xc:] = restricted(HC, lambda j: m[H + X + 2 * j] + m[H + X + 2 * j + 1])
    W = Xc + 2 * HC - 2
    mid = mc[1:1 + W]
    coarse_masks = edge_masks((W, Zc, Yc), 1, 2)
    cw[0] = 0.125 * (mid + mc[2:2 + W])
    cw[1] = 0.125 * (mid + mc[0:W])
    total = cw[0] + cw[1]
    for k, (mask, s) in enumerate(zip(coarse_masks, shifts(mid, 1, 2))):
        total = total + 0.125 * (mid + jnp.where(mask, s, 0.0))
        cw[2 + k] = jnp.where(mask, 0.125 * (mid + s), 0.0)
    cw[6] = jnp.where(mid > 0.0, OMEGA / jnp.where(mid > 0.0, total, 1.0), 0.0)

    def flux(p, i):
        v = p[i]
        zu, zl, yu, yl = shifts(v, 0, 1)
        s = wx[i] * p[i + 1] + wx[i - 1] * p[i - 1]
        s = s + (wzu[i] * zu + wzl[i] * zl)
        return v, s + (wyu[i] * yu + wyl[i] * yl)

    def smooth(src, dst, lo, hi):
        def one(i):
            v, s = flux(src, i)
            dst[i] = (1.0 - OMEGA) * v + rd[i] * (t[i] + s)

        planes(lo, hi, one)

    def residual(p, i):
        v, s = flux(p, i)
        return t[i] - dg[i] * v + s

    first = H - 2 * (HC - 1)

    def leftover(p, lo, hi):
        fill(lo, hi, lambda j: residual(p, first + 2 * j) + residual(p, first + 2 * j + 1))

    def coarse_correct(p):
        left = averaged(W)
        v = cw[6] * left
        for _ in range(SWEEPS - 1):
            zu, zl, yu, yl = shifts(v, 1, 2)
            s = cw[0] * x_up(v) + cw[1] * x_down(v) + (cw[2] * zu + cw[3] * zl) + (cw[4] * yu + cw[5] * yl)
            v = (1.0 - OMEGA) * v + cw[6] * (left + s)
        prolonged(v[HC - 2:W - (HC - 2)])

        def add(j):
            c = rs[rows_at(j, Z), :]
            for h in range(2):
                p[H - 2 + 2 * j + h] = p[H - 2 + 2 * j + h] + c

        planes(0, Xc + 2, add, 5)

    t_x.wait()
    mc_x.start()
    cs_x.start()

    def first_guess(i):
        pa[i] = rd[i] * t[i]

    planes(1, X + 2 * H - 1, first_guess)
    leftover(pa, 0, W)
    coarse_correct(pa)
    smooth(pa, pb, H, H + X)
    p_x.start()

    smooth(pb, pa, H + 1, H + X - 1)
    leftover(pa, HC, HC + Xc - 2)
    def coarse_steps(v, times):
        for _ in range(2 * times):
            length = v.shape[0] - 2
            off = (Xc + 2 * hm - length) // 2
            mid = v[1:-1]
            inner = [jnp.where(k, 1.0, 0.0) for k in edge_masks((1, Zc, Yc), 1, 2)]
            zu, zl, yu, yl = [a * b for a, b in zip(shifts(mid, 1, 2), inner)]
            s = v[2:] + v[:-2] + (zu + zl) + (yu + yl)
            v = mid + (RATE * mcw[off:off + length]) * (s - 6.0 * mid)
        return v

    mc_x.wait()
    cs_x.wait()
    for d in range(C):
        part[0, d] = jnp.where(tm == 0, 0.0, coarse_steps(csw[d], 1))
    p_x.wait()
    smooth(pb, pa, 1, H + 1)
    smooth(pb, pa, H + X - 1, X + 2 * H - 1)
    leftover(pa, 0, HC)
    leftover(pa, HC + Xc - 2, W)
    coarse_correct(pa)
    smooth(pa, pc, H - 1, H + X + 1)

    stages, starts = [], []
    for s in spans:
        starts.append(sum(stages))
        stages.append(max(1, -(-2 * s // Xc)))

    def hop(r, d, target):
        return pltpu.make_async_remote_copy(
            part.at[r, d], vb.at[starts[r], d, pl.ds(hm, Xc)], ss.at[r, d], sr.at[r, d],
            device_id={"tm": target}, device_id_type=MESH)

    def send(r, d):
        if r < R:
            @pl.when(tm + spans[r] < ntm)
            def _():
                hop(r, d, tm + spans[r]).start()

    def sides(r, q, d):
        k = starts[r] + q
        return Exchange([(lambda f, w: vb.at[k, d, pl.ds(f, w)], hm, 2 * spans[r] // stages[r])],
                        fs.at[k, d], fr.at[k, d], Xc)

    direct = [4 * s <= Xc for s in spans]

    def halo(r, side, target):
        h, k = 2 * spans[r], starts[r]
        src, dst = ((0, hm + Xc), (Xc - h, hm - h))[side]
        return pltpu.make_async_remote_copy(
            part.at[r, :, pl.ds(src, h)], vb.at[k, :, pl.ds(dst, h)], hs.at[r, side], hr.at[r, side],
            device_id={"tm": target, "space": me + (-1, 1)[side]}, device_id_type=MESH)

    def send_halo(r):
        if r < R and direct[r]:
            s = spans[r]
            for side, beside in enumerate((has_left, has_right)):
                @pl.when(jnp.logical_and(tm + s < ntm, beside))
                def _():
                    halo(r, side, tm + s).start()

    def advance(r, d):
        times = spans[r] // stages[r]
        for q in range(stages[r]):
            if not direct[r]:
                sides(r, q, d).wait()
            v = coarse_steps(vb[starts[r] + q, d, hm - 2 * times:hm + Xc + 2 * times], times)
            if q + 1 < stages[r]:
                vb[starts[r] + q + 1, d, hm:hm + Xc] = v
                sides(r, q + 1, d).start()
        part[r + 1, d] = part[r, d] + v
        send(r + 1, d)

    def finish(d, i):
        if d == 1:
            grad = pc[i + 1] - pc[i - 1]
        else:
            zu, zl, yu, yl = masked_shifts(pc[i], fine_masks, 0, 1)
            grad = zu - zl if d == 0 else yu - yl
        out[d, i - H] = pr[d, i - H + 1] - 0.5 * m[i] * grad

    for d in range(C):
        planes(H, H + X, lambda i: finish(d, i))
        fill(0, Xc, lambda j: out[d, 2 * j] + out[d, 2 * j + 1])
        ce[d] = averaged(Xc)
        part[0, d] = ce[d] - part[0, d]
        send(0, d)
    send_halo(0)
    for r, s in enumerate(spans):
        @pl.when(tm < s)
        def _():
            for d in range(C):
                part[r + 1, d] = part[r, d]
                send(r + 1, d)
            send_halo(r + 1)

        @pl.when(tm >= s)
        def _():
            if direct[r]:
                for side, beside in enumerate((has_right, has_left)):
                    @pl.when(beside)
                    def _():
                        halo(r, side, tm).wait_recv()

                for d in range(C):
                    hop(r, d, tm).wait_recv()
                    advance(r, d)
            else:
                for d in range(C):
                    hop(r, d, tm).wait_recv()
                    sides(r, 0, d).start()
                for d in range(C):
                    advance(r, d)
            send_halo(r + 1)

    prolonged((part[R] - ce[...]).reshape(C * Xc, Zc, Yc))
    for d in range(C):
        def add(j):
            c = rs[rows_at(d * Xc + j, Z), :]
            for h in range(2):
                out[d, 2 * j + h] = out[d, 2 * j + h] + c

        planes(0, Xc, add, 4)

    for r, s in enumerate(spans):
        @pl.when(tm + s < ntm)
        def _():
            for d in range(C):
                hop(r, d, tm + s).wait_send()
        if direct[r]:
            for side, beside in enumerate((has_left, has_right)):
                @pl.when(jnp.logical_and(tm + s < ntm, beside))
                def _():
                    halo(r, side, tm + s).wait_send()


def body(n, ntm, start_states, labels):
    C, Z, X, Y = start_states.shape[1:]
    Xc, Zc, Yc = X // 2, Z // 2, Y // 2
    HC = H // 2
    spans = []
    while (1 << len(spans)) < ntm:
        spans.append(1 << len(spans))
    wide = pltpu.VMEM((X + 2 * H, Z, Y), f32)
    W = Xc + 2 * HC - 2
    hm = min(2 * max(spans + [1]), Xc)
    total = sum(max(1, -(-2 * s // Xc)) for s in spans) or 1
    rows = max(W, Xc + 2, C * Xc) * Z
    R = len(spans)
    dma = pltpu.SemaphoreType.DMA
    scratch = [
        pltpu.VMEM((C, Z, X, Y), f32), pltpu.VMEM((Z, X, Y), jnp.int32),
        pltpu.VMEM((C, X + 4, Z, Y), f32), wide, pltpu.VMEM((C, X + 2, Z, Y), f32),
        wide, wide, wide, wide, wide, wide, wide, wide, wide, wide, wide,
        pltpu.VMEM((rows, Y), f32), pltpu.VMEM((rows, Yc), f32),
        pltpu.VMEM((Xc + 2 * HC, Zc, Yc), f32), pltpu.VMEM((7, W, Zc, Yc), f32),
        pltpu.VMEM((C, Xc, Zc, Yc), f32), pltpu.VMEM((Xc + 2 * hm, Zc, Yc), f32),
        pltpu.VMEM((C, Xc + 4, Zc, Yc), f32), pltpu.VMEM((R + 1, C, Xc, Zc, Yc), f32),
        pltpu.VMEM((total, C, Xc + 2 * hm, Zc, Yc), f32),
        pltpu.VMEM((Y, Yc), jnp.bfloat16), pltpu.VMEM((Yc, Y), jnp.bfloat16),
        dma((2,)), dma((2, C)), dma((2, C)), dma((2, 1)), dma((2, 1)), dma((2, 1)), dma((2, 1)),
        dma((2, 1)), dma((2, 1)), dma((2, 1)), dma((2, 1)), dma((2, 1)), dma((2, 1)),
        dma((max(R, 1), C)), dma((max(R, 1), C)), dma((total, C, 2, 1)), dma((total, C, 2, 1)),
        dma((max(R, 1), 2)), dma((max(R, 1), 2)),
    ]
    result = pl.pallas_call(
        functools.partial(kernel, n, ntm, spans),
        out_shape=jax.ShapeDtypeStruct((C, X, Z, Y), f32),
        in_specs=[pl.BlockSpec(memory_space=pltpu.HBM)] * 2,
        out_specs=pl.BlockSpec(memory_space=pltpu.VMEM),
        scratch_shapes=scratch,
        compiler_params=pltpu.CompilerParams(
            collective_id=0, has_side_effects=True, vmem_limit_bytes=60 * 1024 * 1024),
    )(start_states[0], labels)
    return jnp.swapaxes(result, 1, 2)[None]


def solution(mesh):
    in_specs = (P("tm", None, None, "space", None), P(None, "space", None))
    out_specs = P("tm", None, None, "space", None)
    fn = functools.partial(body, mesh.shape["space"], mesh.shape["tm"])
    return jax.shard_map(fn, mesh=mesh, in_specs=in_specs, out_specs=out_specs, check_vma=False)
```
